512 devices in a mesh: dp: 2 (over x_lo), row: 8 (over z), col: 32 (over y, x_hi, core).
Axes of the slice: x: 4 (x_hi: 2, x_lo: 2; x = x_hi * 2 + x_lo), y: 8, z: 8, core: 2. Of those that a mesh axis runs over, the one named last changes fastest.
Arguments:
- tokens: bfloat16 [512, 8192], P(('dp', 'col'), 'row'), may hold values from -6 to 6
- gate_weight: bfloat16 [8192, 14336], P('row', 'col'), may hold values from -0.0625 to 0.0625
- up_weight: bfloat16 [8192, 14336], P('row', 'col'), may hold values from -0.0625 to 0.0625
- down_weight: bfloat16 [14336, 8192], P('col', 'row'), may hold values from -0.046875 to 0.046875
- cotangent: bfloat16 [512, 8192], P(('dp', 'col'), 'row'), may hold values from -6 to 6
Outputs:
- layer_output: bfloat16 [512, 8192], P(('dp', 'col'), 'row')
- grad_input: bfloat16 [512, 8192], P(('dp', 'col'), 'row')
- grad_gate: bfloat16 [8192, 14336], P('row', 'col')
- grad_up: bfloat16 [8192, 14336], P('row', 'col')
The draws below stay inside these ranges and needn't reach their ends.
All inputs are finite; a program needn't handle non-finite values.
Results may differ from the reference program's by a relative error of at most 0.02.
Values may be sent and summed in bfloat16 or wider, within the bound.
A program may use at most 64 MiB of HBM per device.

```python
import jax
import jax.numpy as jnp

D = 8192
FF = 14336
TOK_REP = 256
TOKENS = 512
N_DP = 2


def levels(own_key, dims, split, low, high):
    def one(position, blocks):
        heights = jax.random.uniform(jax.random.fold_in(jax.random.fold_in(own_key, 6), position), (blocks,), jnp.float32, low / len(split), high / len(split))
        return jnp.repeat(jnp.exp(heights), dims[position] // blocks).reshape((-1,) + (1,) * (len(dims) - position - 1))

    level = one(*split[0])
    for cut in split[1:]:
        level = level * one(*cut)
    return level


def gaussian(key, extent, scale, limit, shards=(), kind=jnp.bfloat16):
    level = levels(key, extent, shards, -0.22, 0.18) if shards else 1.0
    drawn = jax.random.normal(key, extent, jnp.float32) * scale * level
    return jnp.minimum(jnp.maximum(drawn, -limit), limit).astype(kind)


def setup_inputs(seed: int = 0) -> dict:
    keys = jax.random.split(jax.random.key(seed), 6)
    return {
        "tokens": gaussian(keys[0], (TOKENS, D), 1.0, 6.0, ((0, 64), (1, 8))),
        "gate_weight": gaussian(keys[1], (D, FF), D ** -0.5, 0.0625, ((0, 8), (1, 32))),
        "up_weight": gaussian(keys[2], (D, FF), D ** -0.5, 0.0625, ((0, 8), (1, 32))),
        "down_weight": gaussian(keys[3], (FF, D), FF ** -0.5, 0.046875, ((0, 32), (1, 8))),
        "cotangent": gaussian(keys[4], (TOKENS, D), 1.0, 6.0, ((0, 64), (1, 8))),
    }


def reference(tokens, gate_weight, up_weight, down_weight, cotangent):
    gate_pre = jnp.dot(tokens, gate_weight, preferred_element_type=jnp.float32)
    up_pre = jnp.dot(tokens, up_weight, preferred_element_type=jnp.float32)
    hidden = (jax.nn.silu(gate_pre) * up_pre).astype(jnp.bfloat16)
    layer_output = jnp.dot(hidden, down_weight, preferred_element_type=jnp.float32).astype(jnp.bfloat16)
    grad_hidden = jnp.dot(cotangent, down_weight.T, preferred_element_type=jnp.float32)
    sigmoid_gate = jax.nn.sigmoid(gate_pre)
    grad_gate_pre = (grad_hidden * up_pre * sigmoid_gate * (1.0 + gate_pre * (1.0 - sigmoid_gate))).astype(jnp.bfloat16)
    grad_up_pre = (grad_hidden * jax.nn.silu(gate_pre)).astype(jnp.bfloat16)
    grad_input = (jnp.dot(grad_gate_pre, gate_weight.T, preferred_element_type=jnp.float32)
                  + jnp.dot(grad_up_pre, up_weight.T, preferred_element_type=jnp.float32)).astype(jnp.bfloat16)
    total_gate = jnp.zeros(gate_weight.shape, jnp.float32)
    total_up = jnp.zeros(up_weight.shape, jnp.float32)
    for replica in range(N_DP):
        lower_row = replica * TOK_REP
        replica_tokens = tokens[lower_row:lower_row + TOK_REP]
        replica_gate = jnp.dot(replica_tokens.T, grad_gate_pre[lower_row:lower_row + TOK_REP], preferred_element_type=jnp.float32).astype(jnp.bfloat16)
        replica_up = jnp.dot(replica_tokens.T, grad_up_pre[lower_row:lower_row + TOK_REP], preferred_element_type=jnp.float32).astype(jnp.bfloat16)
        total_gate = total_gate + replica_gate.astype(jnp.float32)
        total_up = total_up + replica_up.astype(jnp.float32)
    return layer_output, grad_input, total_gate.astype(jnp.bfloat16), total_up.astype(jnp.bfloat16)
```

```python
import functools

import jax
import jax.numpy as jnp
from jax import lax
from jax.experimental import pallas as pl
from jax.experimental.pallas import tpu as pltpu
from jax.sharding import PartitionSpec as P

MESH = pl.DeviceIdType.MESH
F32, BF16 = jnp.float32, jnp.bfloat16

GROUPS = {}
N_SEM = 0
for _name, _count in (
    ("tok", 16), ("cot", 16), ("tok_sib", 2), ("cot_sib", 2), ("zgu", 8), ("zgh", 8), ("agu", 8), ("agh", 8),
    ("px", 1), ("pu", 1), ("ph", 1), ("lo_sib", 1), ("gi_sib", 1), ("lo", 16), ("gi", 16),
):
    GROUPS[_name] = N_SEM
    N_SEM += _count


def dot(a, b):
    return lax.dot_general(a, b, (((1,), (0,)), ((), ())), preferred_element_type=F32)


def dot_nt(a, b):
    return lax.dot_general(a, b, (((1,), (1,)), ((), ())), preferred_element_type=F32)


def dot_tn(a, b):
    return lax.dot_general(a, b, (((0,), (0,)), ((), ())), preferred_element_type=F32)


def join(a, b):
    return jnp.concatenate([a[:, :384], b[:, :384], a[:, 384:], b[:, 384:]], axis=1)


def part(x):
    tail = x[:, 768:896]
    return (
        jnp.concatenate([x[:, :384], tail], axis=1),
        jnp.concatenate([x[:, 384:768], pltpu.roll(tail, 64, 1)], axis=1),
    )


def fold(x):
    return jnp.concatenate([x[:, :512], x[:, 512:]], axis=0)


def kernel(
    tok_ref, wg_hbm, wu_hbm, wd_hbm, cot_ref,
    lo_out, gi_out, gg_out, gu_out,
    wg, wu, wd, gx, gc, x, cx, px, sgu, rgu, sgh, rgh, agu, agh, pu, ph,
    hid, gg, gu, part_f, lo_s, lo_i, gi_s, gi_i, lo_t, lo_r, gi_t, gi_r,
    send, recv, wsem,
):
    dp, r, c = lax.axis_index("dp"), lax.axis_index("row"), lax.axis_index("col")
    k = lax.rem(c, 2)
    xh = lax.rem(c // 2, 2)
    y = c // 4
    sib = (dp, r, c + 1 - 2 * k)
    peer = (1 - dp, r, c)
    my_q = r // 2 + 4 * lax.rem(r, 2)

    def chip(j):
        q, dx = j // 2, lax.rem(j, 2)
        odd = lax.rem(q, 2)
        dy = odd * ((q + 1) // 2) + (1 - odd) * (8 - q // 2)
        back = jnp.where(q == 0, 0, jnp.where(q == 7, 7, q - 1 + 2 * odd))
        to = (lax.rem(y + dy, 8) * 2 + lax.rem(xh + dx, 2)) * 2 + k
        return (dp, r, to), back * 2 + dx

    def ring(i):
        odd = lax.rem(i, 2)
        return lax.rem(r + odd * ((i + 1) // 2) + (1 - odd) * (8 - i // 2), 8)

    def copy(src, dst, s, d, to):
        return pltpu.make_async_remote_copy(
            src_ref=src, dst_ref=dst, send_sem=send.at[s], recv_sem=recv.at[d], device_id=to, device_id_type=MESH
        )

    def arrived(dst, d):
        pltpu.make_async_copy(dst, dst, recv.at[d]).wait()

    def left(src, s):
        pltpu.make_async_copy(src, src, send.at[s]).wait()

    def loop(lo, hi, body):
        def step(i, carry):
            body(i)
            return carry
        lax.fori_loop(lo, hi, step, 0)

    loads = [
        pltpu.make_async_copy(a, b, wsem.at[i]) for i, (a, b) in enumerate(((wg_hbm, wg), (wu_hbm, wu), (wd_hbm, wd)))
    ]
    for load in loads:
        load.start()

    barrier = pltpu.get_barrier_semaphore()

    def greet(to):
        pl.semaphore_signal(barrier, inc=1, device_id=to, device_id_type=MESH)

    loop(1, 16, lambda j: greet(chip(j)[0]))
    loop(1, 8, lambda i: greet((dp, ring(i), c)))
    greet(sib)
    greet(peer)
    gx[k, 0] = fold(tok_ref[...].astype(F32)).astype(BF16)
    gc[k, 0] = fold(cot_ref[...].astype(F32)).astype(BF16)
    pl.semaphore_wait(barrier, 24)

    def spread(buf, base):
        def one(j):
            to, slot = chip(j)
            copy(buf.at[k, 0], buf.at[k, slot], base + j, base + slot, to).start()
        loop(1, 16, one)

    spread(gx, GROUPS["tok"])
    spread(gc, GROUPS["cot"])

    def collect(buf, rows, half, base, sib_base):
        lo = 8 * half
        loop(max(lo, 1), lo + 8, lambda j: arrived(buf.at[k, j], base + j))
        mine = buf.at[k, pl.ds(lo, 8)]
        copy(mine, mine, sib_base + half, sib_base + half, sib).start()
        theirs = buf.at[1 - k, pl.ds(lo, 8)]
        arrived(theirs, sib_base + half)

        def unfold(q):
            for core in range(2):
                a, b = buf[core, 2 * q].astype(F32), buf[core, 2 * q + 1].astype(F32)
                left_half = jnp.concatenate([a[:8], b[:8]], axis=0)
                right_half = jnp.concatenate([a[8:], b[8:]], axis=0)
                at = pl.ds(pl.multiple_of(32 * q + 16 * core, 16), 16)
                rows[at, :512] = left_half.astype(BF16)
                rows[at, 512:] = right_half.astype(BF16)
        loop(4 * half, 4 * half + 4, unfold)

    def scatter(src, dst, half, base):
        def one(i):
            to = lax.rem((r // 2) * 2 + 2 * i + half, 8)

            @pl.when(to != r)
            def _():
                copy(src.at[to], dst.at[r], base + to, base + r, (dp, to, c)).start()

            @pl.when(to == r)
            def _():
                dst[r] = src[r]
        loop(0, 4, one)

    for half in range(2):
        collect(gx, x, half, GROUPS["tok"], GROUPS["tok_sib"])
        if half == 0:
            loads[0].wait()
            loads[1].wait()
        lhs = x[128 * half:128 * half + 128]
        gate, up = dot(lhs, wg[...]), dot(lhs, wu[...])
        for i in range(4):
            at = slice(32 * i, 32 * i + 32)
            sgu[2 * i + half] = join(gate[at], up[at]).astype(BF16)
        scatter(sgu, rgu, half, GROUPS["zgu"])
    copy(x, px, GROUPS["px"], GROUPS["px"], peer).start()
    for half in range(2):
        collect(gc, cx, half, GROUPS["cot"], GROUPS["cot_sib"])
        if half == 0:
            loads[2].wait()
        back = dot_nt(cx[128 * half:128 * half + 128], wd[...])
        for i in range(4):
            sgh[2 * i + half] = join(back[32 * i:32 * i + 16], back[32 * i + 16:32 * i + 32]).astype(BF16)
        scatter(sgh, rgh, half, GROUPS["zgh"])

    def reduce_and_share(parts, whole, base, share_base):
        loop(1, 8, lambda i: arrived(parts.at[ring(i)], base + ring(i)))
        total = parts[0].astype(F32)
        for i in range(1, 8):
            total = total + parts[i].astype(F32)
        whole[my_q] = total.astype(BF16)

        def one(i):
            to = ring(i)
            copy(whole.at[my_q], whole.at[my_q], share_base + to, share_base + r, (dp, to, c)).start()
        loop(1, 8, one)

    def gathered(whole, share_base):
        def one(i):
            of = ring(i)
            arrived(whole.at[of // 2 + 4 * lax.rem(of, 2)], share_base + of)
        loop(1, 8, one)

    reduce_and_share(rgu, agu, GROUPS["zgu"], GROUPS["agu"])
    reduce_and_share(rgh, agh, GROUPS["zgh"], GROUPS["agh"])

    def to_sibling(kept, given, name):
        def one(q):
            kept[q] = part_f[pl.ds(pl.multiple_of(32 * q + 16 * (1 - k), 16), 16), :].astype(BF16)
        loop(0, 8, one)
        copy(kept, given, GROUPS[name], GROUPS[name], sib).start()

    def to_owners(given, folded, landed, name, base):
        arrived(given, GROUPS[name])

        def one(q):
            tile = part_f[pl.ds(pl.multiple_of(32 * q + 16 * k, 16), 16), :] + given[q].astype(F32)
            for dx in range(2):
                folded[2 * q + dx] = fold(tile[8 * dx:8 * dx + 8]).astype(BF16)
                to, slot = chip(2 * q + dx)

                @pl.when(2 * q + dx > 0)
                def _():
                    copy(folded.at[2 * q + dx], landed.at[slot], base + 2 * q + dx, base + slot, to).start()
        loop(0, 8, one)
        landed[0] = folded[0]

    def finish(landed, out, base):
        loop(1, 16, lambda j: arrived(landed.at[j], base + j))
        total = landed[0].astype(F32)
        for j in range(1, 16):
            total = total + landed[j].astype(F32)
        out[...] = jnp.concatenate([total[:8], total[8:]], axis=1).astype(out.dtype)

    gathered(agu, GROUPS["agu"])
    copy(agu, pu, GROUPS["pu"], GROUPS["pu"], peer).start()

    def forward(q):
        gate, up = part(agu[q].astype(F32))
        hidden = gate * jax.nn.sigmoid(gate) * up
        hid[pl.ds(pl.multiple_of(32 * q, 32), 32), :] = hidden[:, :448].astype(BF16)
    loop(0, 8, forward)
    part_f[...] = dot(hid[...], wd[...])
    to_sibling(lo_s, lo_i, "lo_sib")
    to_owners(lo_i, lo_t, lo_r, "lo_sib", GROUPS["lo"])

    def backward(joined, halves, first):
        def one(q):
            gate, up = part(joined[q].astype(F32))
            grad = jnp.concatenate(part(halves[q].astype(F32)), axis=0)
            sig = jax.nn.sigmoid(gate)
            at = pl.ds(pl.multiple_of(first + 32 * q, 32), 32)
            gg[at, :] = (grad * up * sig * (1.0 + gate * (1.0 - sig)))[:, :448].astype(BF16)
            gu[at, :] = (grad * (gate * sig))[:, :448].astype(BF16)
        loop(0, 8, one)

    gathered(agh, GROUPS["agh"])
    copy(agh, ph, GROUPS["ph"], GROUPS["ph"], peer).start()
    backward(agu, agh, 0)
    part_f[...] = dot_nt(gg[:256], wg[...]) + dot_nt(gu[:256], wu[...])
    to_sibling(gi_s, gi_i, "gi_sib")
    to_owners(gi_i, gi_t, gi_r, "gi_sib", GROUPS["gi"])
    finish(lo_r, lo_out, GROUPS["lo"])

    arrived(px, GROUPS["px"])
    arrived(pu, GROUPS["pu"])
    arrived(ph, GROUPS["ph"])
    backward(pu, ph, 256)

    def weights(i):
        at = pl.ds(pl.multiple_of(256 * i, 256), 256)
        for grad, out in ((gg, gg_out), (gu, gu_out)):
            out[at, :] = (dot_tn(x[:, at], grad[:256]) + dot_tn(px[:, at], grad[256:])).astype(BF16)
    loop(0, 4, weights)
    finish(gi_r, gi_out, GROUPS["gi"])

    def drain(j):
        left(gx.at[k, 0], GROUPS["tok"] + j)
        left(gc.at[k, 0], GROUPS["cot"] + j)
        left(lo_t.at[j], GROUPS["lo"] + j)
        left(gi_t.at[j], GROUPS["gi"] + j)
    loop(1, 16, drain)

    def drain_row(i):
        to = ring(i)
        left(sgu.at[to], GROUPS["zgu"] + to)
        left(sgh.at[to], GROUPS["zgh"] + to)
        left(agu.at[my_q], GROUPS["agu"] + to)
        left(agh.at[my_q], GROUPS["agh"] + to)
    loop(1, 8, drain_row)
    for half in range(2):
        left(gx.at[k, pl.ds(8 * half, 8)], GROUPS["tok_sib"] + half)
        left(gc.at[k, pl.ds(8 * half, 8)], GROUPS["cot_sib"] + half)
    left(x, GROUPS["px"])
    left(agu, GROUPS["pu"])
    left(agh, GROUPS["ph"])
    left(lo_s, GROUPS["lo_sib"])
    left(gi_s, GROUPS["gi_sib"])


def body(tokens, gate_weight, up_weight, down_weight, cotangent):
    vmem = pl.BlockSpec(memory_space=pltpu.VMEM)
    anywhere = pl.BlockSpec(memory_space=pl.ANY)
    scratch = [
        ((1024, 448), BF16), ((1024, 448), BF16), ((448, 1024), BF16),
        ((2, 16, 16, 512), BF16), ((2, 16, 16, 512), BF16),
        ((256, 1024), BF16), ((256, 1024), BF16), ((256, 1024), BF16),
        ((8, 32, 896), BF16), ((8, 32, 896), BF16), ((8, 16, 896), BF16), ((8, 16, 896), BF16),
        ((8, 32, 896), BF16), ((8, 16, 896), BF16), ((8, 32, 896), BF16), ((8, 16, 896), BF16),
        ((256, 448), BF16), ((512, 448), BF16), ((512, 448), BF16),
        ((256, 1024), F32),
        ((8, 16, 1024), BF16), ((8, 16, 1024), BF16), ((8, 16, 1024), BF16), ((8, 16, 1024), BF16),
        ((16, 16, 512), BF16), ((16, 16, 512), BF16), ((16, 16, 512), BF16), ((16, 16, 512), BF16),
    ]
    return pl.pallas_call(
        kernel,
        out_shape=(
            jax.ShapeDtypeStruct((8, 1024), BF16),
            jax.ShapeDtypeStruct((8, 1024), BF16),
            jax.ShapeDtypeStruct((1024, 448), BF16),
            jax.ShapeDtypeStruct((1024, 448), BF16),
        ),
        in_specs=[vmem, anywhere, anywhere, anywhere, vmem],
        out_specs=(vmem, vmem, vmem, vmem),
        scratch_shapes=[pltpu.VMEM(shape, kind) for shape, kind in scratch]
        + [pltpu.SemaphoreType.DMA((N_SEM,)), pltpu.SemaphoreType.DMA((N_SEM,)), pltpu.SemaphoreType.DMA((3,))],
        compiler_params=pltpu.CompilerParams(
            collective_id=0, has_side_effects=True, vmem_limit_bytes=48 * 1024 * 1024
        ),
        cost_estimate=pl.CostEstimate(flops=2400000000, bytes_accessed=5000000, transcendentals=250000),
        name="swiglu_block",
    )(tokens, gate_weight, up_weight, down_weight, cotangent)


def solution(mesh):
    return jax.shard_map(
        body,
        mesh=mesh,
        in_specs=(
            P(("dp", "col"), "row"),
            P("row", "col"),
            P("row", "col"),
            P("col", "row"),
            P(("dp", "col"), "row"),
        ),
        out_specs=(
            P(("dp", "col"), "row"),
            P(("dp", "col"), "row"),
            P("row", "col"),
            P("row", "col"),
        ),
        check_vma=False,
    )
```

```python
import functools

import jax
import jax.numpy as jnp
from jax import lax
from jax.experimental import pallas as pl
from jax.experimental.pallas import tpu as pltpu
from jax.sharding import PartitionSpec as P

MESH = pl.DeviceIdType.MESH
F32, BF16 = jnp.float32, jnp.bfloat16

GROUPS = {}
N_SEM = 0
for _name, _count in (
    ("tok", 16), ("cot", 16), ("tok_sib", 2), ("cot_sib", 2), ("zgu", 8), ("zgh", 8), ("agu", 8), ("agh", 8),
    ("px", 1), ("px_sib", 1), ("pg", 8), ("lo_sib", 2), ("gi_sib", 2), ("lo", 16), ("gi", 16),
):
    GROUPS[_name] = N_SEM
    N_SEM += _count


def dot(a, b):
    return lax.dot_general(a, b, (((1,), (0,)), ((), ())), preferred_element_type=F32)


def dot_nt(a, b):
    return lax.dot_general(a, b, (((1,), (1,)), ((), ())), preferred_element_type=F32)


def dot_tn(a, b):
    return lax.dot_general(a, b, (((0,), (0,)), ((), ())), preferred_element_type=F32)


def join(a, b):
    return jnp.concatenate([a[:, :384], b[:, :384], a[:, 384:448], b[:, 384:448]], axis=1)


def part(x):
    tail = x[:, 768:896]
    return (
        jnp.concatenate([x[:, :384], tail], axis=1),
        jnp.concatenate([x[:, 384:768], pltpu.roll(tail, 64, 1)], axis=1),
    )


def fold(x):
    return jnp.concatenate([x[:, :512], x[:, 512:]], axis=0)


def kernel(
    tok_ref, wg_hbm, wu_hbm, wd_hbm, cot_ref,
    x_out, g_out, lo_out, gi_out,
    wj, wd, gx, gc, gp, x, cx, sgu, rgu, lgu, cgu, sgh, rgh, lgh, cgh, agu, agh,
    hid, gl, g, lo_f, gi_f, lo_s, lo_i, gi_s, gi_i, lo_t, lo_r, gi_t, gi_r,
    send, recv, wsem,
):
    dp, r, c = lax.axis_index("dp"), lax.axis_index("row"), lax.axis_index("col")
    k = lax.rem(c, 2)
    xh = lax.rem(c // 2, 2)
    y = c // 4
    odd_row = lax.rem(r, 2)
    sib = (dp, r, c + 1 - 2 * k)
    peer = (1 - dp, r, c)

    def chip(j):
        q, dx = j // 2, lax.rem(j, 2)
        odd = lax.rem(q, 2)
        dy = odd * ((q + 1) // 2) + (1 - odd) * (8 - q // 2)
        back = jnp.where(q == 0, 0, jnp.where(q == 7, 7, q - 1 + 2 * odd))
        to = (lax.rem(y + dy, 8) * 2 + lax.rem(xh + dx, 2)) * 2 + k
        return (dp, r, to), back * 2 + dx

    def at_row(offset):
        return lax.rem(r + offset + 8, 8)

    def row_device(offset):
        return (dp, at_row(offset), c)

    def group_of(row):
        return row // 2 + 4 * lax.rem(row, 2)

    def ring(i):
        odd = lax.rem(i, 2)
        return lax.rem(r + odd * ((i + 1) // 2) + (1 - odd) * (8 - i // 2), 8)

    def copy(src, dst, s, d, to):
        return pltpu.make_async_remote_copy(
            src_ref=src, dst_ref=dst, send_sem=send.at[s], recv_sem=recv.at[d], device_id=to, device_id_type=MESH
        )

    def arrived(dst, d):
        pltpu.make_async_copy(dst, dst, recv.at[d]).wait()

    def left(src, s):
        pltpu.make_async_copy(src, src, send.at[s]).wait()

    def loop(lo, hi, body):
        def step(i, carry):
            body(i)
            return carry
        lax.fori_loop(lo, hi, step, 0)

    def rows(start, count):
        return pl.ds(pl.multiple_of(start, count), count)

    loads = [
        pltpu.make_async_copy(a, b, wsem.at[i])
        for i, (a, b) in enumerate((
            (wg_hbm.at[:384], wj.at[:384]),
            (wu_hbm.at[:384], wj.at[384:768]),
            (wg_hbm.at[384:], wj.at[768:832]),
            (wu_hbm.at[384:], wj.at[832:]),
            (wd_hbm, wd),
        ))
    ]
    for load in loads:
        load.start()

    barrier = pltpu.get_barrier_semaphore()

    def greet(to):
        pl.semaphore_signal(barrier, inc=1, device_id=to, device_id_type=MESH)

    loop(1, 16, lambda j: greet(chip(j)[0]))
    loop(1, 5, lambda i: greet((dp, ring(i), c)))
    greet(sib)
    greet(peer)
    gx[k, 0] = fold(tok_ref[...].astype(F32)).astype(BF16)
    gc[k, 0] = fold(cot_ref[...].astype(F32)).astype(BF16)
    pl.semaphore_wait(barrier, 21)

    def spread(buf, base):
        def one(j):
            to, slot = chip(j)
            copy(buf.at[k, 0], buf.at[k, slot], base + j, base + slot, to).start()
        loop(1, 16, one)

    spread(gx, GROUPS["tok"])
    spread(gc, GROUPS["cot"])

    def unfold(buf, into, first, q):
        for core in range(2):
            a, b = buf[core, 2 * q].astype(F32), buf[core, 2 * q + 1].astype(F32)
            at = rows(first + 32 * q + 16 * core, 16)
            into[at, :512] = jnp.concatenate([a[:8], b[:8]], axis=0).astype(BF16)
            into[at, 512:] = jnp.concatenate([a[8:], b[8:]], axis=0).astype(BF16)

    def collect(buf, into, half, base, sib_base):
        lo = 8 * half
        loop(max(lo, 1), lo + 8, lambda j: arrived(buf.at[k, j], base + j))
        mine = buf.at[k, pl.ds(lo, 8)]
        copy(mine, mine, sib_base + half, sib_base + half, sib).start()
        arrived(buf.at[1 - k, pl.ds(lo, 8)], sib_base + half)
        loop(4 * half, 4 * half + 4, lambda q: unfold(buf, into, 0, q))

    def scatter(src, near, far, half, base):
        @pl.when(odd_row == half)
        def _():
            copy(src.at[at_row(4)], far.at[2], base + 6, base + 6, row_device(2 + 4 * odd_row)).start()

        @pl.when(odd_row != half)
        def _():
            copy(src.at[at_row(3)], far.at[0], base + 4, base + 4, row_device(1)).start()
            copy(src.at[at_row(-3)], far.at[1], base + 5, base + 5, row_device(-1)).start()
            copy(src.at[at_row(1)], near.at[0], base, base, row_device(1)).start()
            copy(src.at[at_row(-1)], near.at[1], base + 1, base + 1, row_device(-1)).start()

    def relay(src, near, far, both, base, parity):
        @pl.when(odd_row == parity)
        def _():
            for i in range(3):
                arrived(far.at[i], base + 4 + i)
            third = far[2].astype(F32)
            up_sum = src[at_row(2)].astype(F32) + far[0].astype(F32)
            down_sum = src[at_row(-2)].astype(F32) + far[1].astype(F32)
            if parity == 0:
                up_sum = up_sum + third
            else:
                down_sum = down_sum + third
            both[0] = up_sum.astype(BF16)
            both[1] = down_sum.astype(BF16)
            copy(both.at[0], near.at[2], base + 2, base + 2, row_device(2)).start()
            copy(both.at[1], near.at[3], base + 3, base + 3, row_device(-2)).start()

    def reduce_and_share(src, near, whole, base, share):
        for i in range(4):
            arrived(near.at[i], base + i)
        total = src[r].astype(F32)
        for i in range(4):
            total = total + near[i].astype(F32)
        own = group_of(r)
        whole[own] = total.astype(BF16)
        block = whole.at[own]
        copy(block, block, share + 3, share + 4, row_device(2)).start()
        copy(block, block, share + 4, share + 3, row_device(-2)).start()
        copy(block, block, share + 1, share + 2, row_device(1)).start()
        copy(block, block, share + 2, share + 1, row_device(-1)).start()

    def pass_on(whole, share):
        above, below = whole.at[group_of(at_row(2))], whole.at[group_of(at_row(-2))]
        arrived(above, share + 3)
        arrived(below, share + 4)
        copy(below, below, share + 5, share + 6, row_device(1)).start()
        copy(above, above, share + 6, share + 5, row_device(-1)).start()
        last = whole.at[group_of(at_row(6 + 4 * odd_row))]
        copy(last, last, share + 7, share + 7, row_device(2 + 4 * odd_row)).start()

    def come(whole, share, lo, hi):
        loop(lo, hi, lambda i: arrived(whole.at[group_of(ring(i))], share + i))

    for half in range(2):
        collect(gx, x, half, GROUPS["tok"], GROUPS["tok_sib"])
        if half == 0:
            for load in loads[:4]:
                load.wait()
        pre = dot_nt(x[128 * half:128 * half + 128], wj[...])
        for i in range(4):
            sgu[2 * i + half] = pre[32 * i:32 * i + 32].astype(BF16)
        scatter(sgu, rgu, lgu, half, GROUPS["zgu"])
    copy(gx.at[k], gp.at[k], GROUPS["px"], GROUPS["px"], peer).start()
    relay(sgu, rgu, lgu, cgu, GROUPS["zgu"], 0)
    for half in range(2):
        collect(gc, cx, half, GROUPS["cot"], GROUPS["cot_sib"])
        if half == 0:
            loads[4].wait()
        back = dot_nt(cx[128 * half:128 * half + 128], wd[...])
        for i in range(4):
            sgh[2 * i + half] = join(back[32 * i:32 * i + 16], back[32 * i + 16:32 * i + 32]).astype(BF16)
        scatter(sgh, rgh, lgh, half, GROUPS["zgh"])
        if half == 0:
            relay(sgu, rgu, lgu, cgu, GROUPS["zgu"], 1)
    relay(sgh, rgh, lgh, cgh, GROUPS["zgh"], 0)
    reduce_and_share(sgu, rgu, agu, GROUPS["zgu"], GROUPS["agu"])
    relay(sgh, rgh, lgh, cgh, GROUPS["zgh"], 1)
    reduce_and_share(sgh, rgh, agh, GROUPS["zgh"], GROUPS["agh"])
    arrived(gp.at[k], GROUPS["px"])
    copy(gp.at[k], gp.at[k], GROUPS["px_sib"], GROUPS["px_sib"], sib).start()

    def to_sibling(sums, kept, given, turn, name):
        def one(i):
            kept[i] = sums[rows(32 * i + 16 * (1 - k), 16), :].astype(BF16)
        loop(4 * turn, 4 * turn + 4, one)
        some = pl.ds(4 * turn, 4)
        copy(kept.at[some], given.at[some], GROUPS[name] + turn, GROUPS[name] + turn, sib).start()

    def to_owners(sums, given, folded, landed, turn, name, base):
        arrived(given.at[pl.ds(4 * turn, 4)], GROUPS[name] + turn)

        def one(i):
            tile = sums[rows(32 * i + 16 * k, 16), :] + given[i].astype(F32)
            q = group_of(ring(i))
            for dx in range(2):
                j = 2 * q + dx
                block = fold(tile[8 * dx:8 * dx + 8]).astype(BF16)

                @pl.when(j == 0)
                def _():
                    landed[0] = block

                @pl.when(j > 0)
                def _():
                    folded[j] = block
                    to, slot = chip(j)
                    copy(folded.at[j], landed.at[slot], base + j, base + slot, to).start()
        loop(4 * turn, 4 * turn + 4, one)

    def forward(turn):
        def one(i):
            gate, up = part(agu[group_of(ring(i))].astype(F32))
            hidden = gate * jax.nn.sigmoid(gate) * up
            hid[rows(32 * i, 32), :] = hidden[:, :448].astype(BF16)
        loop(4 * turn, 4 * turn + 4, one)
        lines = slice(128 * turn, 128 * turn + 128)
        lo_f[lines] = dot(hid[lines], wd[...])
        to_sibling(lo_f, lo_s, lo_i, turn, "lo_sib")

    def backward(turn):
        def one(i):
            q = group_of(ring(i))
            gate, up = part(agu[q].astype(F32))
            grad = jnp.concatenate(part(agh[q].astype(F32)), axis=0)
            sig = jax.nn.sigmoid(gate)
            both = join(grad * up * sig * (1.0 + gate * (1.0 - sig)), grad * (gate * sig)).astype(BF16)
            gl[rows(32 * i, 32), :] = both
            g[rows(32 * q, 32), :] = both
            copy(
                g.at[rows(32 * q, 32)], g.at[rows(256 + 32 * q, 32)], GROUPS["pg"] + q, GROUPS["pg"] + q, peer
            ).start()
        loop(4 * turn, 4 * turn + 4, one)
        lines = slice(128 * turn, 128 * turn + 128)
        gi_f[lines] = dot(gl[lines], wj[...])
        to_sibling(gi_f, gi_s, gi_i, turn, "gi_sib")

    pass_on(agu, GROUPS["agu"])
    come(agu, GROUPS["agu"], 1, 3)
    forward(0)
    pass_on(agh, GROUPS["agh"])
    come(agh, GROUPS["agh"], 1, 3)
    backward(0)
    to_owners(lo_f, lo_i, lo_t, lo_r, 0, "lo_sib", GROUPS["lo"])
    to_owners(gi_f, gi_i, gi_t, gi_r, 0, "gi_sib", GROUPS["gi"])
    come(agu, GROUPS["agu"], 5, 8)
    forward(1)
    come(agh, GROUPS["agh"], 5, 8)
    backward(1)
    to_owners(lo_f, lo_i, lo_t, lo_r, 1, "lo_sib", GROUPS["lo"])
    to_owners(gi_f, gi_i, gi_t, gi_r, 1, "gi_sib", GROUPS["gi"])

    arrived(gp.at[1 - k], GROUPS["px_sib"])
    loop(0, 8, lambda q: unfold(gp, x, 256, q))
    save_x = pltpu.make_async_copy(x, x_out, wsem.at[5])
    save_x.start()
    loop(1, 16, lambda j: arrived(lo_r.at[j], GROUPS["lo"] + j))
    save_lo = pltpu.make_async_copy(lo_r, lo_out, wsem.at[6])
    save_lo.start()
    loop(0, 8, lambda q: arrived(g.at[rows(256 + 32 * q, 32)], GROUPS["pg"] + q))
    save_g = pltpu.make_async_copy(g, g_out, wsem.at[7])
    save_g.start()
    loop(1, 16, lambda j: arrived(gi_r.at[j], GROUPS["gi"] + j))
    save_gi = pltpu.make_async_copy(gi_r, gi_out, wsem.at[8])
    save_gi.start()

    def drain(j):
        left(gx.at[k, 0], GROUPS["tok"] + j)
        left(gc.at[k, 0], GROUPS["cot"] + j)
        left(lo_t.at[j], GROUPS["lo"] + j)
        left(gi_t.at[j], GROUPS["gi"] + j)
    loop(1, 16, drain)

    def drain_row(i):
        left(sgu.at[0], GROUPS["zgu"] + i)
        left(sgh.at[0], GROUPS["zgh"] + i)
        left(agu.at[0], GROUPS["agu"] + i + 1)
        left(agh.at[0], GROUPS["agh"] + i + 1)
    loop(0, 7, drain_row)
    loop(0, 8, lambda q: left(g.at[rows(32 * q, 32)], GROUPS["pg"] + q))
    for half in range(2):
        left(gx.at[k, pl.ds(8 * half, 8)], GROUPS["tok_sib"] + half)
        left(gc.at[k, pl.ds(8 * half, 8)], GROUPS["cot_sib"] + half)
        left(lo_s.at[pl.ds(4 * half, 4)], GROUPS["lo_sib"] + half)
        left(gi_s.at[pl.ds(4 * half, 4)], GROUPS["gi_sib"] + half)
    left(gx.at[k], GROUPS["px"])
    left(gp.at[k], GROUPS["px_sib"])
    for save in (save_x, save_lo, save_g, save_gi):
        save.wait()


def finish(x_ref, g_ref, lo_ref, gi_ref, lo_out, gi_out, gg_out, gu_out):
    for parts, out in ((lo_ref, lo_out), (gi_ref, gi_out)):
        total = parts[0].astype(F32)
        for j in range(1, 16):
            total = total + parts[j].astype(F32)
        out[...] = jnp.concatenate([total[:8], total[8:]], axis=1).astype(BF16)
    grads = dot_tn(g_ref[...], x_ref[...]).astype(BF16)
    gg_out[:384] = grads[:384]
    gu_out[:384] = grads[384:768]
    gg_out[384:] = grads[768:832]
    gu_out[384:] = grads[832:]


def body(tokens, gate_weight, up_weight, down_weight, cotangent):
    vmem = pl.BlockSpec(memory_space=pltpu.VMEM)
    anywhere = pl.BlockSpec(memory_space=pl.ANY)
    scratch = [
        ((896, 1024), BF16), ((448, 1024), BF16),
        ((2, 16, 16, 512), BF16), ((2, 16, 16, 512), BF16), ((2, 16, 16, 512), BF16),
        ((512, 1024), BF16), ((256, 1024), BF16),
        ((8, 32, 896), BF16), ((4, 32, 896), BF16), ((3, 32, 896), BF16), ((2, 32, 896), BF16),
        ((8, 16, 896), BF16), ((4, 16, 896), BF16), ((3, 16, 896), BF16), ((2, 16, 896), BF16),
        ((8, 32, 896), BF16), ((8, 16, 896), BF16),
        ((256, 448), BF16), ((256, 896), BF16), ((512, 896), BF16),
        ((256, 1024), F32), ((256, 1024), F32),
        ((8, 16, 1024), BF16), ((8, 16, 1024), BF16), ((8, 16, 1024), BF16), ((8, 16, 1024), BF16),
        ((16, 16, 512), BF16), ((16, 16, 512), BF16), ((16, 16, 512), BF16), ((16, 16, 512), BF16),
    ]
    grant = 61 * 1024 * 1024
    x, g, lo, gi = pl.pallas_call(
        kernel,
        out_shape=(
            jax.ShapeDtypeStruct((512, 1024), BF16),
            jax.ShapeDtypeStruct((512, 896), BF16),
            jax.ShapeDtypeStruct((16, 16, 512), BF16),
            jax.ShapeDtypeStruct((16, 16, 512), BF16),
        ),
        in_specs=[vmem, anywhere, anywhere, anywhere, vmem],
        out_specs=(anywhere,) * 4,
        scratch_shapes=[pltpu.VMEM(shape, kind) for shape, kind in scratch]
        + [pltpu.SemaphoreType.DMA((N_SEM,)), pltpu.SemaphoreType.DMA((N_SEM,)), pltpu.SemaphoreType.DMA((9,))],
        compiler_params=pltpu.CompilerParams(collective_id=0, has_side_effects=True, vmem_limit_bytes=grant),
        cost_estimate=pl.CostEstimate(flops=1500000000, bytes_accessed=5000000, transcendentals=250000),
        name="swiglu_block",
    )(tokens, gate_weight.T, up_weight.T, down_weight, cotangent)
    layer_output, grad_input, grad_gate, grad_up = pl.pallas_call(
        finish,
        out_shape=(
            jax.ShapeDtypeStruct((8, 1024), BF16),
            jax.ShapeDtypeStruct((8, 1024), BF16),
            jax.ShapeDtypeStruct((448, 1024), BF16),
            jax.ShapeDtypeStruct((448, 1024), BF16),
        ),
        in_specs=[vmem] * 4,
        out_specs=(vmem,) * 4,
        compiler_params=pltpu.CompilerParams(vmem_limit_bytes=grant),
        cost_estimate=pl.CostEstimate(flops=940000000, bytes_accessed=4500000, transcendentals=0),
        name="finish",
    )(x, g, lo, gi)
    return layer_output, grad_input, grad_gate.T, grad_up.T


def solution(mesh):
    return jax.shard_map(
        body,
        mesh=mesh,
        in_specs=(
            P(("dp", "col"), "row"),
            P("row", "col"),
            P("row", "col"),
            P("col", "row"),
            P(("dp", "col"), "row"),
        ),
        out_specs=(
            P(("dp", "col"), "row"),
            P(("dp", "col"), "row"),
            P("row", "col"),
            P("row", "col"),
        ),
        check_vma=False,
    )
```

```python
import functools

import jax
import jax.numpy as jnp
from jax import lax
from jax.experimental import pallas as pl
from jax.experimental.pallas import tpu as pltpu
from jax.sharding import PartitionSpec as P

MESH = pl.DeviceIdType.MESH
F32, BF16 = jnp.float32, jnp.bfloat16

GROUPS = {}
N_SEM = 0
for _name, _count in (
    ("tok", 16), ("cot", 16), ("tok_sib", 2), ("cot_sib", 2), ("zgu", 8), ("zgh", 8), ("agu", 8), ("agh", 8),
    ("px", 1), ("px_sib", 1), ("pg", 8), ("lo_sib", 2), ("gi_sib", 2), ("lo", 16), ("gi", 16),
):
    GROUPS[_name] = N_SEM
    N_SEM += _count


def dot(a, b):
    return lax.dot_general(a, b, (((1,), (0,)), ((), ())), preferred_element_type=F32)


def dot_nt(a, b):
    return lax.dot_general(a, b, (((1,), (1,)), ((), ())), preferred_element_type=F32)


def dot_tn(a, b):
    return lax.dot_general(a, b, (((0,), (0,)), ((), ())), preferred_element_type=F32)


def join(a, b):
    return jnp.concatenate([a[:, :384], b[:, :384], a[:, 384:448], b[:, 384:448]], axis=1)


def part(x):
    tail = x[:, 768:896]
    return (
        jnp.concatenate([x[:, :384], tail], axis=1),
        jnp.concatenate([x[:, 384:768], pltpu.roll(tail, 64, 1)], axis=1),
    )


def fold(x):
    return jnp.concatenate([x[:, :512], x[:, 512:]], axis=0)


def kernel(
    tok_ref, wg_hbm, wu_hbm, wd_hbm, cot_ref,
    x_out, g_out, lo_out, gi_out,
    wj, wd, gx, gc, gp, x, cx, sgu, rgu, lgu, cgu, sgh, rgh, lgh, cgh, agu, agh,
    hid, gl, g, lo_f, gi_f, lo_s, lo_i, gi_s, gi_i, lo_t, lo_r, gi_t, gi_r,
    send, recv, wsem,
):
    dp, r, c = lax.axis_index("dp"), lax.axis_index("row"), lax.axis_index("col")
    k = lax.rem(c, 2)
    xh = lax.rem(c // 2, 2)
    y = c // 4
    odd_row = lax.rem(r, 2)
    sib = (dp, r, c + 1 - 2 * k)
    peer = (1 - dp, r, c)

    def chip(j):
        q, dx = j // 2, lax.rem(j, 2)
        odd = lax.rem(q, 2)
        dy = odd * ((q + 1) // 2) + (1 - odd) * (8 - q // 2)
        back = jnp.where(q == 0, 0, jnp.where(q == 7, 7, q - 1 + 2 * odd))
        to = (lax.rem(y + dy, 8) * 2 + lax.rem(xh + dx, 2)) * 2 + k
        return (dp, r, to), back * 2 + dx

    def at_row(offset):
        return lax.rem(r + offset + 8, 8)

    def row_device(offset):
        return (dp, at_row(offset), c)

    def group_of(row):
        return row // 2 + 4 * lax.rem(row, 2)

    def ring(i):
        odd = lax.rem(i, 2)
        return lax.rem(r + odd * ((i + 1) // 2) + (1 - odd) * (8 - i // 2), 8)

    def copy(src, dst, s, d, to):
        return pltpu.make_async_remote_copy(
            src_ref=src, dst_ref=dst, send_sem=send.at[s], recv_sem=recv.at[d], device_id=to, device_id_type=MESH
        )

    def arrived(dst, d):
        pltpu.make_async_copy(dst, dst, recv.at[d]).wait()

    def left(src, s):
        pltpu.make_async_copy(src, src, send.at[s]).wait()

    def loop(lo, hi, body):
        def step(i, carry):
            body(i)
            return carry
        lax.fori_loop(lo, hi, step, 0)

    def rows(start, count):
        return pl.ds(pl.multiple_of(start, count), count)

    loads = [
        pltpu.make_async_copy(a, b, wsem.at[i])
        for i, (a, b) in enumerate((
            (wg_hbm.at[:384], wj.at[:384]),
            (wu_hbm.at[:384], wj.at[384:768]),
            (wg_hbm.at[384:], wj.at[768:832]),
            (wu_hbm.at[384:], wj.at[832:]),
            (wd_hbm, wd),
        ))
    ]
    for load in loads:
        load.start()

    barrier = pltpu.get_barrier_semaphore()

    def greet(to):
        pl.semaphore_signal(barrier, inc=1, device_id=to, device_id_type=MESH)

    loop(1, 16, lambda j: greet(chip(j)[0]))
    loop(1, 5, lambda i: greet((dp, ring(i), c)))
    greet(sib)
    greet(peer)
    gx[k, 0] = fold(tok_ref[...].astype(F32)).astype(BF16)
    gc[k, 0] = fold(cot_ref[...].astype(F32)).astype(BF16)
    pl.semaphore_wait(barrier, 21)

    def spread(buf, base):
        def one(j):
            to, slot = chip(16 - j)
            copy(buf.at[k, 0], buf.at[k, slot], base + 16 - j, base + slot, to).start()
        loop(1, 16, one)

    spread(gx, GROUPS["tok"])
    spread(gc, GROUPS["cot"])

    def unfold(buf, into, first, q):
        for core in range(2):
            a, b = buf[core, 2 * q].astype(F32), buf[core, 2 * q + 1].astype(F32)
            at = rows(first + 32 * q + 16 * core, 16)
            into[at, :512] = jnp.concatenate([a[:8], b[:8]], axis=0).astype(BF16)
            into[at, 512:] = jnp.concatenate([a[8:], b[8:]], axis=0).astype(BF16)

    def pair_up(buf, base, sib_base):
        for half in (1, 0):
            lo = 8 * half
            loop(max(lo, 1), lo + 8, lambda j: arrived(buf.at[k, j], base + j))
            mine = buf.at[k, pl.ds(lo, 8)]
            copy(mine, mine, sib_base + half, sib_base + half, sib).start()

    def collect(buf, into, half, sib_base):
        arrived(buf.at[1 - k, pl.ds(8 * half, 8)], sib_base + half)
        loop(4 * half, 4 * half + 4, lambda q: unfold(buf, into, 0, q))

    def scatter(src, near, far, half, base):
        @pl.when(odd_row == half)
        def _():
            copy(src.at[at_row(4)], far.at[2], base + 6, base + 6, row_device(2 + 4 * odd_row)).start()

        @pl.when(odd_row != half)
        def _():
            copy(src.at[at_row(3)], far.at[0], base + 4, base + 4, row_device(1)).start()
            copy(src.at[at_row(-3)], far.at[1], base + 5, base + 5, row_device(-1)).start()
            copy(src.at[at_row(1)], near.at[0], base, base, row_device(1)).start()
            copy(src.at[at_row(-1)], near.at[1], base + 1, base + 1, row_device(-1)).start()

    def relay(src, near, far, both, base, parity):
        @pl.when(odd_row == parity)
        def _():
            for i in range(3):
                arrived(far.at[i], base + 4 + i)
            third = far[2].astype(F32)
            up_sum = src[at_row(2)].astype(F32) + far[0].astype(F32)
            down_sum = src[at_row(-2)].astype(F32) + far[1].astype(F32)
            if parity == 0:
                up_sum = up_sum + third
            else:
                down_sum = down_sum + third
            both[0] = up_sum.astype(BF16)
            both[1] = down_sum.astype(BF16)
            copy(both.at[0], near.at[2], base + 2, base + 2, row_device(2)).start()
            copy(both.at[1], near.at[3], base + 3, base + 3, row_device(-2)).start()

    def reduce_and_share(src, near, whole, base, share):
        for i in range(4):
            arrived(near.at[i], base + i)
        total = src[r].astype(F32)
        for i in range(4):
            total = total + near[i].astype(F32)
        own = group_of(r)
        whole[own] = total.astype(BF16)
        block = whole.at[own]
        copy(block, block, share + 3, share + 4, row_device(2)).start()
        copy(block, block, share + 4, share + 3, row_device(-2)).start()
        copy(block, block, share + 1, share + 2, row_device(1)).start()
        copy(block, block, share + 2, share + 1, row_device(-1)).start()

    def pass_on(whole, share):
        above, below = whole.at[group_of(at_row(2))], whole.at[group_of(at_row(-2))]
        arrived(above, share + 3)
        arrived(below, share + 4)
        copy(below, below, share + 5, share + 6, row_device(1)).start()
        copy(above, above, share + 6, share + 5, row_device(-1)).start()
        last = whole.at[group_of(at_row(6 + 4 * odd_row))]
        copy(last, last, share + 7, share + 7, row_device(2 + 4 * odd_row)).start()

    def come(whole, share, lo, hi):
        loop(lo, hi, lambda i: arrived(whole.at[group_of(ring(i))], share + i))

    pair_up(gx, GROUPS["tok"], GROUPS["tok_sib"])
    for half in (1, 0):
        collect(gx, x, half, GROUPS["tok_sib"])
        if half == 1:
            for load in loads[:4]:
                load.wait()
        pre = dot_nt(x[128 * half:128 * half + 128], wj[...])
        for i in range(4):
            sgu[2 * i + half] = pre[32 * i:32 * i + 32].astype(BF16)
        scatter(sgu, rgu, lgu, half, GROUPS["zgu"])
    copy(gx.at[k], gp.at[k], GROUPS["px"], GROUPS["px"], peer).start()
    relay(sgu, rgu, lgu, cgu, GROUPS["zgu"], 1)
    relay(sgu, rgu, lgu, cgu, GROUPS["zgu"], 0)
    pair_up(gc, GROUPS["cot"], GROUPS["cot_sib"])
    for half in (1, 0):
        collect(gc, cx, half, GROUPS["cot_sib"])
        if half == 1:
            loads[4].wait()
        back = dot_nt(cx[128 * half:128 * half + 128], wd[...])
        for i in range(4):
            sgh[2 * i + half] = join(back[32 * i:32 * i + 16], back[32 * i + 16:32 * i + 32]).astype(BF16)
        scatter(sgh, rgh, lgh, half, GROUPS["zgh"])
    relay(sgh, rgh, lgh, cgh, GROUPS["zgh"], 1)
    relay(sgh, rgh, lgh, cgh, GROUPS["zgh"], 0)
    reduce_and_share(sgu, rgu, agu, GROUPS["zgu"], GROUPS["agu"])
    reduce_and_share(sgh, rgh, agh, GROUPS["zgh"], GROUPS["agh"])
    arrived(gp.at[k], GROUPS["px"])
    copy(gp.at[k], gp.at[k], GROUPS["px_sib"], GROUPS["px_sib"], sib).start()

    first, last = (0, 5), (5, 8)

    def to_sibling(sums, kept, given, turn, name):
        def one(i):
            kept[i] = sums[rows(32 * i + 16 * (1 - k), 16), :].astype(BF16)
        lo, hi = (first, last)[turn]
        loop(lo, hi, one)
        some = pl.ds(lo, hi - lo)
        copy(kept.at[some], given.at[some], GROUPS[name] + turn, GROUPS[name] + turn, sib).start()

    def to_owners(sums, given, folded, landed, turn, name, base):
        lo, hi = (first, last)[turn]
        arrived(given.at[pl.ds(lo, hi - lo)], GROUPS[name] + turn)

        def one(step):
            q = 7 - step
            offset = lax.rem(2 * lax.rem(q, 4) + q // 4 - r + 8, 8)
            i = jnp.where(offset == 0, 0, jnp.where(offset <= 4, 2 * offset - 1, 16 - 2 * offset))

            @pl.when((i >= lo) & (i < hi))
            def _():
                tile = sums[rows(32 * i + 16 * k, 16), :] + given[i].astype(F32)
                for dx in (1, 0):
                    j = 2 * q + dx
                    block = fold(tile[8 * dx:8 * dx + 8]).astype(BF16)

                    @pl.when(j == 0)
                    def _():
                        landed[0] = block

                    @pl.when(j > 0)
                    def _():
                        folded[j] = block
                        to, slot = chip(j)
                        copy(folded.at[j], landed.at[slot], base + j, base + slot, to).start()
        loop(0, 8, one)

    def forward(turn):
        def one(i):
            gate, up = part(agu[group_of(ring(i))].astype(F32))
            hidden = gate * jax.nn.sigmoid(gate) * up
            hid[rows(32 * i, 32), :] = hidden[:, :448].astype(BF16)
        lo, hi = (first, last)[turn]
        loop(lo, hi, one)
        lines = slice(32 * lo, 32 * hi)
        lo_f[lines] = dot(hid[lines], wd[...])
        to_sibling(lo_f, lo_s, lo_i, turn, "lo_sib")

    def backward(turn):
        def one(i):
            q = group_of(ring(i))
            gate, up = part(agu[q].astype(F32))
            grad = jnp.concatenate(part(agh[q].astype(F32)), axis=0)
            sig = jax.nn.sigmoid(gate)
            both = join(grad * up * sig * (1.0 + gate * (1.0 - sig)), grad * (gate * sig)).astype(BF16)
            gl[rows(32 * i, 32), :] = both
            g[rows(32 * q, 32), :] = both
            copy(
                g.at[rows(32 * q, 32)], g.at[rows(256 + 32 * q, 32)], GROUPS["pg"] + q, GROUPS["pg"] + q, peer
            ).start()
        lo, hi = (first, last)[turn]
        loop(lo, hi, one)
        lines = slice(32 * lo, 32 * hi)
        gi_f[lines] = dot(gl[lines], wj[...])
        to_sibling(gi_f, gi_s, gi_i, turn, "gi_sib")

    pass_on(agu, GROUPS["agu"])
    come(agu, GROUPS["agu"], 1, 3)
    forward(0)
    pass_on(agh, GROUPS["agh"])
    come(agh, GROUPS["agh"], 1, 3)
    backward(0)
    to_owners(lo_f, lo_i, lo_t, lo_r, 0, "lo_sib", GROUPS["lo"])
    to_owners(gi_f, gi_i, gi_t, gi_r, 0, "gi_sib", GROUPS["gi"])
    come(agu, GROUPS["agu"], 5, 8)
    forward(1)
    to_owners(lo_f, lo_i, lo_t, lo_r, 1, "lo_sib", GROUPS["lo"])
    come(agh, GROUPS["agh"], 5, 8)
    backward(1)
    to_owners(gi_f, gi_i, gi_t, gi_r, 1, "gi_sib", GROUPS["gi"])

    arrived(gp.at[1 - k], GROUPS["px_sib"])
    loop(0, 8, lambda q: unfold(gp, x, 256, q))
    save_x = pltpu.make_async_copy(x, x_out, wsem.at[5])
    save_x.start()
    loop(1, 16, lambda j: arrived(lo_r.at[j], GROUPS["lo"] + j))
    save_lo = pltpu.make_async_copy(lo_r, lo_out, wsem.at[6])
    save_lo.start()
    loop(0, 8, lambda q: arrived(g.at[rows(256 + 32 * q, 32)], GROUPS["pg"] + q))
    save_g = pltpu.make_async_copy(g, g_out, wsem.at[7])
    save_g.start()
    loop(1, 16, lambda j: arrived(gi_r.at[j], GROUPS["gi"] + j))
    save_gi = pltpu.make_async_copy(gi_r, gi_out, wsem.at[8])
    save_gi.start()

    def drain(j):
        left(gx.at[k, 0], GROUPS["tok"] + j)
        left(gc.at[k, 0], GROUPS["cot"] + j)
        left(lo_t.at[j], GROUPS["lo"] + j)
        left(gi_t.at[j], GROUPS["gi"] + j)
    loop(1, 16, drain)

    def drain_row(i):
        left(sgu.at[0], GROUPS["zgu"] + i)
        left(sgh.at[0], GROUPS["zgh"] + i)
        left(agu.at[0], GROUPS["agu"] + i + 1)
        left(agh.at[0], GROUPS["agh"] + i + 1)
    loop(0, 7, drain_row)
    loop(0, 8, lambda q: left(g.at[rows(32 * q, 32)], GROUPS["pg"] + q))
    for half in range(2):
        left(gx.at[k, pl.ds(8 * half, 8)], GROUPS["tok_sib"] + half)
        left(gc.at[k, pl.ds(8 * half, 8)], GROUPS["cot_sib"] + half)
        lo, hi = (first, last)[half]
        left(lo_s.at[pl.ds(lo, hi - lo)], GROUPS["lo_sib"] + half)
        left(gi_s.at[pl.ds(lo, hi - lo)], GROUPS["gi_sib"] + half)
    left(gx.at[k], GROUPS["px"])
    left(gp.at[k], GROUPS["px_sib"])
    for save in (save_x, save_lo, save_g, save_gi):
        save.wait()


def finish(x_ref, g_ref, lo_ref, gi_ref, lo_out, gi_out, gg_out, gu_out):
    for parts, out in ((lo_ref, lo_out), (gi_ref, gi_out)):
        total = parts[0].astype(F32)
        for j in range(1, 16):
            total = total + parts[j].astype(F32)
        out[...] = jnp.concatenate([total[:8], total[8:]], axis=1).astype(BF16)
    grads = dot_tn(g_ref[...], x_ref[...]).astype(BF16)
    gg_out[:384] = grads[:384]
    gu_out[:384] = grads[384:768]
    gg_out[384:] = grads[768:832]
    gu_out[384:] = grads[832:]


def body(tokens, gate_weight, up_weight, down_weight, cotangent):
    vmem = pl.BlockSpec(memory_space=pltpu.VMEM)
    anywhere = pl.BlockSpec(memory_space=pl.ANY)
    scratch = [
        ((896, 1024), BF16), ((448, 1024), BF16),
        ((2, 16, 16, 512), BF16), ((2, 16, 16, 512), BF16), ((2, 16, 16, 512), BF16),
        ((512, 1024), BF16), ((256, 1024), BF16),
        ((8, 32, 896), BF16), ((4, 32, 896), BF16), ((3, 32, 896), BF16), ((2, 32, 896), BF16),
        ((8, 16, 896), BF16), ((4, 16, 896), BF16), ((3, 16, 896), BF16), ((2, 16, 896), BF16),
        ((8, 32, 896), BF16), ((8, 16, 896), BF16),
        ((256, 448), BF16), ((256, 896), BF16), ((512, 896), BF16),
        ((256, 1024), F32), ((256, 1024), F32),
        ((8, 16, 1024), BF16), ((8, 16, 1024), BF16), ((8, 16, 1024), BF16), ((8, 16, 1024), BF16),
        ((16, 16, 512), BF16), ((16, 16, 512), BF16), ((16, 16, 512), BF16), ((16, 16, 512), BF16),
    ]
    grant = 61 * 1024 * 1024
    x, g, lo, gi = pl.pallas_call(
        kernel,
        out_shape=(
            jax.ShapeDtypeStruct((512, 1024), BF16),
            jax.ShapeDtypeStruct((512, 896), BF16),
            jax.ShapeDtypeStruct((16, 16, 512), BF16),
            jax.ShapeDtypeStruct((16, 16, 512), BF16),
        ),
        in_specs=[vmem, anywhere, anywhere, anywhere, vmem],
        out_specs=(anywhere,) * 4,
        scratch_shapes=[pltpu.VMEM(shape, kind) for shape, kind in scratch]
        + [pltpu.SemaphoreType.DMA((N_SEM,)), pltpu.SemaphoreType.DMA((N_SEM,)), pltpu.SemaphoreType.DMA((9,))],
        compiler_params=pltpu.CompilerParams(collective_id=0, has_side_effects=True, vmem_limit_bytes=grant),
        cost_estimate=pl.CostEstimate(flops=1500000000, bytes_accessed=5000000, transcendentals=250000),
        name="swiglu_block",
    )(tokens, gate_weight.T, up_weight.T, down_weight, cotangent)
    layer_output, grad_input, grad_gate, grad_up = pl.pallas_call(
        finish,
        out_shape=(
            jax.ShapeDtypeStruct((8, 1024), BF16),
            jax.ShapeDtypeStruct((8, 1024), BF16),
            jax.ShapeDtypeStruct((448, 1024), BF16),
            jax.ShapeDtypeStruct((448, 1024), BF16),
        ),
        in_specs=[vmem] * 4,
        out_specs=(vmem,) * 4,
        compiler_params=pltpu.CompilerParams(vmem_limit_bytes=grant),
        cost_estimate=pl.CostEstimate(flops=940000000, bytes_accessed=4500000, transcendentals=0),
        name="finish",
    )(x, g, lo, gi)
    return layer_output, grad_input, grad_gate.T, grad_up.T


def solution(mesh):
    return jax.shard_map(
        body,
        mesh=mesh,
        in_specs=(
            P(("dp", "col"), "row"),
            P("row", "col"),
            P("row", "col"),
            P("col", "row"),
            P(("dp", "col"), "row"),
        ),
        out_specs=(
            P(("dp", "col"), "row"),
            P(("dp", "col"), "row"),
            P("row", "col"),
            P("row", "col"),
        ),
        check_vma=False,
    )
```

```python
import functools

import jax
import jax.numpy as jnp
from jax import lax
from jax.experimental import pallas as pl
from jax.experimental.pallas import tpu as pltpu
from jax.sharding import PartitionSpec as P

MESH = pl.DeviceIdType.MESH
F32, BF16 = jnp.float32, jnp.bfloat16

GROUPS = {}
N_SEM = 0
for _name, _count in (
    ("tok", 16), ("cot", 16), ("tok_sib", 2), ("cot_sib", 2), ("zgu", 8), ("zgh", 8), ("agu", 8), ("agh", 8),
    ("px", 1), ("px_sib", 1), ("pg", 8), ("lo_sib", 2), ("gi_sib", 2), ("lo", 16), ("gi", 16),
):
    GROUPS[_name] = N_SEM
    N_SEM += _count


def dot(a, b):
    return lax.dot_general(a, b, (((1,), (0,)), ((), ())), preferred_element_type=F32)


def dot_nt(a, b):
    return lax.dot_general(a, b, (((1,), (1,)), ((), ())), preferred_element_type=F32)


def dot_tn(a, b):
    return lax.dot_general(a, b, (((0,), (0,)), ((), ())), preferred_element_type=F32)


def join(a, b):
    return jnp.concatenate([a[:, :384], b[:, :384], a[:, 384:448], b[:, 384:448]], axis=1)


def part(x):
    tail = x[:, 768:896]
    return (
        jnp.concatenate([x[:, :384], tail], axis=1),
        jnp.concatenate([x[:, 384:768], pltpu.roll(tail, 64, 1)], axis=1),
    )


def fold(x):
    return jnp.concatenate([x[:, :512], x[:, 512:]], axis=0)


def kernel(
    tok_ref, wg_hbm, wu_hbm, wd_hbm, cot_ref,
    x_out, g_out, lo_out, gi_out,
    wj, wd, gx, gc, gp, x, cx, sgu, rgu, lgu, cgu, sgh, rgh, lgh, cgh, agu, agh,
    hid, gl, g, lo_f, gi_f, lo_s, lo_i, gi_s, gi_i, lo_t, lo_r, gi_t, gi_r,
    send, recv, wsem,
):
    dp, r, c = lax.axis_index("dp"), lax.axis_index("row"), lax.axis_index("col")
    k = lax.rem(c, 2)
    xh = lax.rem(c // 2, 2)
    y = c // 4
    odd_row = lax.rem(r, 2)
    sib = (dp, r, c + 1 - 2 * k)
    peer = (1 - dp, r, c)

    def chip(j):
        q, dx = j // 2, lax.rem(j, 2)
        odd = lax.rem(q, 2)
        dy = odd * ((q + 1) // 2) + (1 - odd) * (8 - q // 2)
        back = jnp.where(q == 0, 0, jnp.where(q == 7, 7, q - 1 + 2 * odd))
        to = (lax.rem(y + dy, 8) * 2 + lax.rem(xh + dx, 2)) * 2 + k
        return (dp, r, to), back * 2 + dx

    def at_row(offset):
        return lax.rem(r + offset + 8, 8)

    def row_device(offset):
        return (dp, at_row(offset), c)

    def group_of(row):
        return row // 2 + 4 * lax.rem(row, 2)

    def ring(i):
        odd = lax.rem(i, 2)
        return lax.rem(r + odd * ((i + 1) // 2) + (1 - odd) * (8 - i // 2), 8)

    def copy(src, dst, s, d, to):
        return pltpu.make_async_remote_copy(
            src_ref=src, dst_ref=dst, send_sem=send.at[s], recv_sem=recv.at[d], device_id=to, device_id_type=MESH
        )

    def arrived(dst, d):
        pltpu.make_async_copy(dst, dst, recv.at[d]).wait()

    def left(src, s):
        pltpu.make_async_copy(src, src, send.at[s]).wait()

    def loop(lo, hi, body):
        def step(i, carry):
            body(i)
            return carry
        lax.fori_loop(lo, hi, step, 0)

    def rows(start, count):
        return pl.ds(pl.multiple_of(start, count), count)

    loads = [
        pltpu.make_async_copy(a, b, wsem.at[i])
        for i, (a, b) in enumerate((
            (wg_hbm.at[:384], wj.at[:384]),
            (wu_hbm.at[:384], wj.at[384:768]),
            (wg_hbm.at[384:], wj.at[768:832]),
            (wu_hbm.at[384:], wj.at[832:]),
            (wd_hbm, wd),
        ))
    ]
    for load in loads:
        load.start()

    barrier = pltpu.get_barrier_semaphore()

    def greet(to):
        pl.semaphore_signal(barrier, inc=1, device_id=to, device_id_type=MESH)

    loop(1, 16, lambda j: greet(chip(j)[0]))
    loop(1, 5, lambda i: greet((dp, ring(i), c)))
    greet(sib)
    greet(peer)
    gx[k, 0] = fold(tok_ref[...].astype(F32)).astype(BF16)
    gc[k, 0] = fold(cot_ref[...].astype(F32)).astype(BF16)
    pl.semaphore_wait(barrier, 21)

    def spread(buf, base):
        def one(j):
            to, slot = chip(16 - j)
            copy(buf.at[k, 0], buf.at[k, slot], base + 16 - j, base + slot, to).start()
        loop(1, 16, one)

    spread(gx, GROUPS["tok"])

    def unfold(buf, into, first, q):
        for core in range(2):
            a, b = buf[core, 2 * q].astype(F32), buf[core, 2 * q + 1].astype(F32)
            at = rows(first + 32 * q + 16 * core, 16)
            into[at, :512] = jnp.concatenate([a[:8], b[:8]], axis=0).astype(BF16)
            into[at, 512:] = jnp.concatenate([a[8:], b[8:]], axis=0).astype(BF16)

    def pair_up(buf, base, sib_base, halves):
        for half in halves:
            lo = 8 * half
            loop(max(lo, 1), lo + 8, lambda j: arrived(buf.at[k, j], base + j))
            mine = buf.at[k, pl.ds(lo, 8)]
            copy(mine, mine, sib_base + half, sib_base + half, sib).start()

    def collect(buf, into, half, sib_base):
        arrived(buf.at[1 - k, pl.ds(8 * half, 8)], sib_base + half)
        loop(4 * half, 4 * half + 4, lambda q: unfold(buf, into, 0, q))

    def scatter(src, near, far, half, base):
        @pl.when(odd_row == half)
        def _():
            copy(src.at[at_row(4)], far.at[2], base + 6, base + 6, row_device(2 + 4 * odd_row)).start()

        @pl.when(odd_row != half)
        def _():
            copy(src.at[at_row(3)], far.at[0], base + 4, base + 4, row_device(1)).start()
            copy(src.at[at_row(-3)], far.at[1], base + 5, base + 5, row_device(-1)).start()
            copy(src.at[at_row(1)], near.at[0], base, base, row_device(1)).start()
            copy(src.at[at_row(-1)], near.at[1], base + 1, base + 1, row_device(-1)).start()

    def relay(src, near, far, both, base, parity):
        @pl.when(odd_row == parity)
        def _():
            for i in (1 - parity, parity, 2):
                arrived(far.at[i], base + 4 + i)
                if i == parity:
                    continue
                side = 1 - parity if i < 2 else parity
                total = src[at_row(2 - 4 * side)].astype(F32) + far[side].astype(F32)
                if i == 2:
                    total = total + far[2].astype(F32)
                both[side] = total.astype(BF16)
                at = base + 2 + side
                copy(both.at[side], near.at[2 + side], at, at, row_device(2 - 4 * side)).start()

    def reduce_and_share(src, near, whole, base, share):
        for i in range(4):
            arrived(near.at[i], base + i)
        total = src[r].astype(F32)
        for i in range(4):
            total = total + near[i].astype(F32)
        own = group_of(r)
        whole[own] = total.astype(BF16)
        block = whole.at[own]
        copy(block, block, share + 3, share + 4, row_device(2)).start()
        copy(block, block, share + 4, share + 3, row_device(-2)).start()
        copy(block, block, share + 1, share + 2, row_device(1)).start()
        copy(block, block, share + 2, share + 1, row_device(-1)).start()

    def pass_on(whole, share):
        above, below = whole.at[group_of(at_row(2))], whole.at[group_of(at_row(-2))]
        arrived(above, share + 3)
        arrived(below, share + 4)
        copy(below, below, share + 5, share + 6, row_device(1)).start()
        copy(above, above, share + 6, share + 5, row_device(-1)).start()
        last = whole.at[group_of(at_row(6 + 4 * odd_row))]
        copy(last, last, share + 7, share + 7, row_device(2 + 4 * odd_row)).start()

    def come(whole, share, lo, hi):
        loop(lo, hi, lambda i: arrived(whole.at[group_of(ring(i))], share + i))

    pair_up(gx, GROUPS["tok"], GROUPS["tok_sib"], (1,))
    spread(gc, GROUPS["cot"])
    pair_up(gx, GROUPS["tok"], GROUPS["tok_sib"], (0,))
    for half in (1, 0):
        collect(gx, x, half, GROUPS["tok_sib"])
        if half == 1:
            for load in loads[:4]:
                load.wait()
        pre = dot_nt(x[128 * half:128 * half + 128], wj[...])
        for i in range(4):
            sgu[2 * i + half] = pre[32 * i:32 * i + 32].astype(BF16)
        scatter(sgu, rgu, lgu, half, GROUPS["zgu"])
    copy(gx.at[k], gp.at[k], GROUPS["px"], GROUPS["px"], peer).start()
    relay(sgu, rgu, lgu, cgu, GROUPS["zgu"], 1)
    pair_up(gc, GROUPS["cot"], GROUPS["cot_sib"], (1,))
    relay(sgu, rgu, lgu, cgu, GROUPS["zgu"], 0)
    pair_up(gc, GROUPS["cot"], GROUPS["cot_sib"], (0,))
    for half in (1, 0):
        collect(gc, cx, half, GROUPS["cot_sib"])
        if half == 1:
            loads[4].wait()
        back = dot_nt(cx[128 * half:128 * half + 128], wd[...])
        for i in range(4):
            sgh[2 * i + half] = join(back[32 * i:32 * i + 16], back[32 * i + 16:32 * i + 32]).astype(BF16)
        scatter(sgh, rgh, lgh, half, GROUPS["zgh"])
    relay(sgh, rgh, lgh, cgh, GROUPS["zgh"], 1)
    relay(sgh, rgh, lgh, cgh, GROUPS["zgh"], 0)
    reduce_and_share(sgu, rgu, agu, GROUPS["zgu"], GROUPS["agu"])
    reduce_and_share(sgh, rgh, agh, GROUPS["zgh"], GROUPS["agh"])
    arrived(gp.at[k], GROUPS["px"])
    copy(gp.at[k], gp.at[k], GROUPS["px_sib"], GROUPS["px_sib"], sib).start()

    first, last = (0, 5), (5, 8)

    def to_sibling(sums, kept, given, turn, name):
        def one(i):
            kept[i] = sums[rows(32 * i + 16 * (1 - k), 16), :].astype(BF16)
        lo, hi = (first, last)[turn]
        loop(lo, hi, one)
        some = pl.ds(lo, hi - lo)
        copy(kept.at[some], given.at[some], GROUPS[name] + turn, GROUPS[name] + turn, sib).start()

    def to_owners(sums, given, folded, landed, turn, name, base):
        lo, hi = (first, last)[turn]
        arrived(given.at[pl.ds(lo, hi - lo)], GROUPS[name] + turn)

        def one(step):
            q = 7 - step
            offset = lax.rem(2 * lax.rem(q, 4) + q // 4 - r + 8, 8)
            i = jnp.where(offset == 0, 0, jnp.where(offset <= 4, 2 * offset - 1, 16 - 2 * offset))

            @pl.when((i >= lo) & (i < hi))
            def _():
                tile = sums[rows(32 * i + 16 * k, 16), :] + given[i].astype(F32)
                for dx in (1, 0):
                    j = 2 * q + dx
                    block = fold(tile[8 * dx:8 * dx + 8]).astype(BF16)

                    @pl.when(j == 0)
                    def _():
                        landed[0] = block

                    @pl.when(j > 0)
                    def _():
                        folded[j] = block
                        to, slot = chip(j)
                        copy(folded.at[j], landed.at[slot], base + j, base + slot, to).start()
        loop(0, 8, one)

    def forward(turn):
        def one(i):
            gate, up = part(agu[group_of(ring(i))].astype(F32))
            hidden = gate * jax.nn.sigmoid(gate) * up
            hid[rows(32 * i, 32), :] = hidden[:, :448].astype(BF16)
        lo, hi = (first, last)[turn]
        loop(lo, hi, one)
        lines = slice(32 * lo, 32 * hi)
        lo_f[lines] = dot(hid[lines], wd[...])
        to_sibling(lo_f, lo_s, lo_i, turn, "lo_sib")

    def backward(turn):
        def one(i):
            q = group_of(ring(i))
            gate, up = part(agu[q].astype(F32))
            grad = jnp.concatenate(part(agh[q].astype(F32)), axis=0)
            sig = jax.nn.sigmoid(gate)
            both = join(grad * up * sig * (1.0 + gate * (1.0 - sig)), grad * (gate * sig)).astype(BF16)
            gl[rows(32 * i, 32), :] = both
            g[rows(32 * q, 32), :] = both
            copy(
                g.at[rows(32 * q, 32)], g.at[rows(256 + 32 * q, 32)], GROUPS["pg"] + q, GROUPS["pg"] + q, peer
            ).start()
        lo, hi = (first, last)[turn]
        loop(lo, hi, one)
        lines = slice(32 * lo, 32 * hi)
        gi_f[lines] = dot(gl[lines], wj[...])
        to_sibling(gi_f, gi_s, gi_i, turn, "gi_sib")

    pass_on(agu, GROUPS["agu"])
    come(agu, GROUPS["agu"], 1, 3)
    forward(0)
    pass_on(agh, GROUPS["agh"])
    come(agh, GROUPS["agh"], 1, 3)
    backward(0)
    to_owners(lo_f, lo_i, lo_t, lo_r, 0, "lo_sib", GROUPS["lo"])
    to_owners(gi_f, gi_i, gi_t, gi_r, 0, "gi_sib", GROUPS["gi"])
    come(agu, GROUPS["agu"], 5, 8)
    forward(1)
    to_owners(lo_f, lo_i, lo_t, lo_r, 1, "lo_sib", GROUPS["lo"])
    come(agh, GROUPS["agh"], 5, 8)
    backward(1)
    to_owners(gi_f, gi_i, gi_t, gi_r, 1, "gi_sib", GROUPS["gi"])

    arrived(gp.at[1 - k], GROUPS["px_sib"])
    loop(0, 8, lambda q: unfold(gp, x, 256, q))
    save_x = pltpu.make_async_copy(x, x_out, wsem.at[5])
    save_x.start()
    def drain(j):
        left(gx.at[k, 0], GROUPS["tok"] + j)
        left(gc.at[k, 0], GROUPS["cot"] + j)
        left(lo_t.at[j], GROUPS["lo"] + j)
        left(gi_t.at[j], GROUPS["gi"] + j)
    loop(1, 16, drain)

    def drain_row(i):
        left(sgu.at[0], GROUPS["zgu"] + i)
        left(sgh.at[0], GROUPS["zgh"] + i)
        left(agu.at[0], GROUPS["agu"] + i + 1)
        left(agh.at[0], GROUPS["agh"] + i + 1)
    loop(0, 7, drain_row)
    loop(0, 8, lambda q: left(g.at[rows(32 * q, 32)], GROUPS["pg"] + q))
    for half in range(2):
        left(gx.at[k, pl.ds(8 * half, 8)], GROUPS["tok_sib"] + half)
        left(gc.at[k, pl.ds(8 * half, 8)], GROUPS["cot_sib"] + half)
        lo, hi = (first, last)[half]
        left(lo_s.at[pl.ds(lo, hi - lo)], GROUPS["lo_sib"] + half)
        left(gi_s.at[pl.ds(lo, hi - lo)], GROUPS["gi_sib"] + half)
    left(gx.at[k], GROUPS["px"])
    left(gp.at[k], GROUPS["px_sib"])
    loop(1, 16, lambda j: arrived(lo_r.at[j], GROUPS["lo"] + j))
    save_lo = pltpu.make_async_copy(lo_r, lo_out, wsem.at[6])
    save_lo.start()
    loop(0, 8, lambda q: arrived(g.at[rows(256 + 32 * q, 32)], GROUPS["pg"] + q))
    save_g = pltpu.make_async_copy(g, g_out, wsem.at[7])
    save_g.start()

    loop(1, 16, lambda j: arrived(gi_r.at[j], GROUPS["gi"] + j))
    save_gi = pltpu.make_async_copy(gi_r, gi_out, wsem.at[8])
    save_gi.start()
    for save in (save_x, save_lo, save_g, save_gi):
        save.wait()


def finish(x_ref, g_ref, lo_ref, gi_ref, lo_out, gi_out, gg_out, gu_out):
    for parts, out in ((lo_ref, lo_out), (gi_ref, gi_out)):
        total = parts[0].astype(F32)
        for j in range(1, 16):
            total = total + parts[j].astype(F32)
        out[...] = jnp.concatenate([total[:8], total[8:]], axis=1).astype(BF16)
    grads = dot_tn(g_ref[...], x_ref[...]).astype(BF16)
    gg_out[:384] = grads[:384]
    gu_out[:384] = grads[384:768]
    gg_out[384:] = grads[768:832]
    gu_out[384:] = grads[832:]


def body(tokens, gate_weight, up_weight, down_weight, cotangent):
    vmem = pl.BlockSpec(memory_space=pltpu.VMEM)
    anywhere = pl.BlockSpec(memory_space=pl.ANY)
    scratch = [
        ((896, 1024), BF16), ((448, 1024), BF16),
        ((2, 16, 16, 512), BF16), ((2, 16, 16, 512), BF16), ((2, 16, 16, 512), BF16),
        ((512, 1024), BF16), ((256, 1024), BF16),
        ((8, 32, 896), BF16), ((4, 32, 896), BF16), ((3, 32, 896), BF16), ((2, 32, 896), BF16),
        ((8, 16, 896), BF16), ((4, 16, 896), BF16), ((3, 16, 896), BF16), ((2, 16, 896), BF16),
        ((8, 32, 896), BF16), ((8, 16, 896), BF16),
        ((256, 448), BF16), ((256, 896), BF16), ((512, 896), BF16),
        ((256, 1024), F32), ((256, 1024), F32),
        ((8, 16, 1024), BF16), ((8, 16, 1024), BF16), ((8, 16, 1024), BF16), ((8, 16, 1024), BF16),
        ((16, 16, 512), BF16), ((16, 16, 512), BF16), ((16, 16, 512), BF16), ((16, 16, 512), BF16),
    ]
    grant = 61 * 1024 * 1024
    x, g, lo, gi = pl.pallas_call(
        kernel,
        out_shape=(
            jax.ShapeDtypeStruct((512, 1024), BF16),
            jax.ShapeDtypeStruct((512, 896), BF16),
            jax.ShapeDtypeStruct((16, 16, 512), BF16),
            jax.ShapeDtypeStruct((16, 16, 512), BF16),
        ),
        in_specs=[vmem, anywhere, anywhere, anywhere, vmem],
        out_specs=(anywhere,) * 4,
        scratch_shapes=[pltpu.VMEM(shape, kind) for shape, kind in scratch]
        + [pltpu.SemaphoreType.DMA((N_SEM,)), pltpu.SemaphoreType.DMA((N_SEM,)), pltpu.SemaphoreType.DMA((9,))],
        compiler_params=pltpu.CompilerParams(collective_id=0, has_side_effects=True, vmem_limit_bytes=grant),
        cost_estimate=pl.CostEstimate(flops=1500000000, bytes_accessed=5000000, transcendentals=250000),
        name="swiglu_block",
    )(tokens, gate_weight.T, up_weight.T, down_weight, cotangent)
    layer_output, grad_input, grad_gate, grad_up = pl.pallas_call(
        finish,
        out_shape=(
            jax.ShapeDtypeStruct((8, 1024), BF16),
            jax.ShapeDtypeStruct((8, 1024), BF16),
            jax.ShapeDtypeStruct((448, 1024), BF16),
            jax.ShapeDtypeStruct((448, 1024), BF16),
        ),
        in_specs=[vmem] * 4,
        out_specs=(vmem,) * 4,
        compiler_params=pltpu.CompilerParams(vmem_limit_bytes=grant),
        cost_estimate=pl.CostEstimate(flops=940000000, bytes_accessed=4500000, transcendentals=0),
        name="finish",
    )(x, g, lo, gi)
    return layer_output, grad_input, grad_gate.T, grad_up.T


def solution(mesh):
    return jax.shard_map(
        body,
        mesh=mesh,
        in_specs=(
            P(("dp", "col"), "row"),
            P("row", "col"),
            P("row", "col"),
            P("col", "row"),
            P(("dp", "col"), "row"),
        ),
        out_specs=(
            P(("dp", "col"), "row"),
            P(("dp", "col"), "row"),
            P("row", "col"),
            P("row", "col"),
        ),
        check_vma=False,
    )
```

```python
import functools

import jax
import jax.numpy as jnp
from jax import lax
from jax.experimental import pallas as pl
from jax.experimental.pallas import tpu as pltpu
from jax.sharding import PartitionSpec as P

MESH = pl.DeviceIdType.MESH
F32, BF16 = jnp.float32, jnp.bfloat16

GROUPS = {}
N_SEM = 0
for _name, _count in (
    ("tok", 16), ("cot", 16), ("tok_sib", 2), ("cot_sib", 2), ("zgu", 8), ("zgh", 8), ("agu", 8), ("agh", 8),
    ("px", 1), ("px_sib", 1), ("pg", 8), ("lo_sib", 2), ("gi_sib", 2), ("lo", 16), ("gi", 16),
):
    GROUPS[_name] = N_SEM
    N_SEM += _count


def dot(a, b):
    return lax.dot_general(a, b, (((1,), (0,)), ((), ())), preferred_element_type=F32)


def dot_nt(a, b):
    return lax.dot_general(a, b, (((1,), (1,)), ((), ())), preferred_element_type=F32)


def dot_tn(a, b):
    return lax.dot_general(a, b, (((0,), (0,)), ((), ())), preferred_element_type=F32)


def join(a, b):
    return jnp.concatenate([a[:, :384], b[:, :384], a[:, 384:448], b[:, 384:448]], axis=1)


def part(x):
    tail = x[:, 768:896]
    return (
        jnp.concatenate([x[:, :384], tail], axis=1),
        jnp.concatenate([x[:, 384:768], pltpu.roll(tail, 64, 1)], axis=1),
    )


def fold(x):
    return jnp.concatenate([x[:, :512], x[:, 512:]], axis=0)


def kernel(
    tok_ref, wg_hbm, wu_hbm, wd_hbm, cot_ref,
    x_out, g_out, lo_out, gi_out,
    wj, wd, gx, gc, gp, x, cx, sgu, rgu, lgu, cgu, sgh, rgh, lgh, cgh, agu, agh,
    hid, gl, g, lo_f, gi_f, lo_s, lo_i, gi_s, gi_i, lo_t, lo_r, gi_t, gi_r,
    send, recv, wsem,
):
    dp, r, c = lax.axis_index("dp"), lax.axis_index("row"), lax.axis_index("col")
    k = lax.rem(c, 2)
    xh = lax.rem(c // 2, 2)
    y = c // 4
    odd_row = lax.rem(r, 2)
    sib = (dp, r, c + 1 - 2 * k)
    peer = (1 - dp, r, c)

    def chip(j):
        q, dx = j // 2, lax.rem(j, 2)
        odd = lax.rem(q, 2)
        dy = odd * ((q + 1) // 2) + (1 - odd) * (8 - q // 2)
        back = jnp.where(q == 0, 0, jnp.where(q == 7, 7, q - 1 + 2 * odd))
        to = (lax.rem(y + dy, 8) * 2 + lax.rem(xh + dx, 2)) * 2 + k
        return (dp, r, to), back * 2 + dx

    def at_row(offset):
        return lax.rem(r + offset + 8, 8)

    def row_device(offset):
        return (dp, at_row(offset), c)

    def group_of(row):
        return row // 2 + 4 * lax.rem(row, 2)

    def ring(i):
        odd = lax.rem(i, 2)
        return lax.rem(r + odd * ((i + 1) // 2) + (1 - odd) * (8 - i // 2), 8)

    def copy(src, dst, s, d, to):
        return pltpu.make_async_remote_copy(
            src_ref=src, dst_ref=dst, send_sem=send.at[s], recv_sem=recv.at[d], device_id=to, device_id_type=MESH
        )

    def arrived(dst, d):
        pltpu.make_async_copy(dst, dst, recv.at[d]).wait()

    def left(src, s):
        pltpu.make_async_copy(src, src, send.at[s]).wait()

    def loop(lo, hi, body):
        def step(i, carry):
            body(i)
            return carry
        lax.fori_loop(lo, hi, step, 0)

    def rows(start, count):
        return pl.ds(pl.multiple_of(start, count), count)

    loads = [
        pltpu.make_async_copy(a, b, wsem.at[i])
        for i, (a, b) in enumerate((
            (wg_hbm.at[:384], wj.at[:384]),
            (wu_hbm.at[:384], wj.at[384:768]),
            (wg_hbm.at[384:], wj.at[768:832]),
            (wu_hbm.at[384:], wj.at[832:]),
            (wd_hbm, wd),
        ))
    ]
    for load in loads:
        load.start()

    barrier = pltpu.get_barrier_semaphore()

    def greet(to):
        pl.semaphore_signal(barrier, inc=1, device_id=to, device_id_type=MESH)

    loop(1, 16, lambda j: greet(chip(j)[0]))
    loop(1, 5, lambda i: greet((dp, ring(i), c)))
    greet(sib)
    greet(peer)
    gx[k, 0] = fold(tok_ref[...].astype(F32)).astype(BF16)
    gc[k, 0] = fold(cot_ref[...].astype(F32)).astype(BF16)
    pl.semaphore_wait(barrier, 21)

    def spread(buf, base):
        def one(j):
            to, slot = chip(16 - j)
            copy(buf.at[k, 0], buf.at[k, slot], base + 16 - j, base + slot, to).start()
        loop(1, 16, one)

    spread(gx, GROUPS["tok"])

    def unfold(buf, into, first, q):
        for core in range(2):
            a, b = buf[core, 2 * q].astype(F32), buf[core, 2 * q + 1].astype(F32)
            at = rows(first + 32 * q + 16 * core, 16)
            into[at, :512] = jnp.concatenate([a[:8], b[:8]], axis=0).astype(BF16)
            into[at, 512:] = jnp.concatenate([a[8:], b[8:]], axis=0).astype(BF16)

    def pair_up(buf, base, sib_base, halves):
        for half in halves:
            lo = 8 * half
            loop(max(lo, 1), lo + 8, lambda j: arrived(buf.at[k, j], base + j))
            mine = buf.at[k, pl.ds(lo, 8)]
            copy(mine, mine, sib_base + half, sib_base + half, sib).start()

    def collect(buf, into, half, sib_base):
        arrived(buf.at[1 - k, pl.ds(8 * half, 8)], sib_base + half)
        loop(4 * half, 4 * half + 4, lambda q: unfold(buf, into, 0, q))

    def scatter(src, near, far, half, base):
        @pl.when(odd_row == half)
        def _():
            copy(src.at[at_row(4)], far.at[2], base + 6, base + 6, row_device(2 + 4 * odd_row)).start()

        @pl.when(odd_row != half)
        def _():
            copy(src.at[at_row(3)], far.at[0], base + 4, base + 4, row_device(1)).start()
            copy(src.at[at_row(-3)], far.at[1], base + 5, base + 5, row_device(-1)).start()
            copy(src.at[at_row(1)], near.at[0], base, base, row_device(1)).start()
            copy(src.at[at_row(-1)], near.at[1], base + 1, base + 1, row_device(-1)).start()

    def relay(src, near, far, both, base, parity):
        @pl.when(odd_row == parity)
        def _():
            for i in (1 - parity, parity, 2):
                arrived(far.at[i], base + 4 + i)
                if i == parity:
                    continue
                side = 1 - parity if i < 2 else parity
                total = src[at_row(2 - 4 * side)].astype(F32) + far[side].astype(F32)
                if i == 2:
                    total = total + far[2].astype(F32)
                both[side] = total.astype(BF16)
                at = base + 2 + side
                copy(both.at[side], near.at[2 + side], at, at, row_device(2 - 4 * side)).start()

    def reduce_and_share(src, near, whole, base, share):
        for i in range(4):
            arrived(near.at[i], base + i)
        total = src[r].astype(F32)
        for i in range(4):
            total = total + near[i].astype(F32)
        own = group_of(r)
        whole[own] = total.astype(BF16)
        block = whole.at[own]
        copy(block, block, share + 3, share + 4, row_device(2)).start()
        copy(block, block, share + 4, share + 3, row_device(-2)).start()
        copy(block, block, share + 1, share + 2, row_device(1)).start()
        copy(block, block, share + 2, share + 1, row_device(-1)).start()

    def pass_on(whole, share):
        above, below = whole.at[group_of(at_row(2))], whole.at[group_of(at_row(-2))]
        arrived(above, share + 3)
        arrived(below, share + 4)
        copy(below, below, share + 5, share + 6, row_device(1)).start()
        copy(above, above, share + 6, share + 5, row_device(-1)).start()
        last = whole.at[group_of(at_row(6 + 4 * odd_row))]
        copy(last, last, share + 7, share + 7, row_device(2 + 4 * odd_row)).start()

    def come(whole, share, lo, hi):
        loop(lo, hi, lambda i: arrived(whole.at[group_of(ring(i))], share + i))

    pair_up(gx, GROUPS["tok"], GROUPS["tok_sib"], (1,))
    spread(gc, GROUPS["cot"])
    pair_up(gx, GROUPS["tok"], GROUPS["tok_sib"], (0,))
    for half in (1, 0):
        collect(gx, x, half, GROUPS["tok_sib"])
        if half == 1:
            for load in loads[:4]:
                load.wait()
        pre = dot_nt(x[128 * half:128 * half + 128], wj[...])
        for i in range(4):
            sgu[2 * i + half] = pre[32 * i:32 * i + 32].astype(BF16)
        scatter(sgu, rgu, lgu, half, GROUPS["zgu"])
    relay(sgu, rgu, lgu, cgu, GROUPS["zgu"], 1)
    pair_up(gc, GROUPS["cot"], GROUPS["cot_sib"], (1,))
    relay(sgu, rgu, lgu, cgu, GROUPS["zgu"], 0)
    pair_up(gc, GROUPS["cot"], GROUPS["cot_sib"], (0,))
    for half in (1, 0):
        collect(gc, cx, half, GROUPS["cot_sib"])
        if half == 1:
            loads[4].wait()
        back = dot_nt(cx[128 * half:128 * half + 128], wd[...])
        for i in range(4):
            sgh[2 * i + half] = join(back[32 * i:32 * i + 16], back[32 * i + 16:32 * i + 32]).astype(BF16)
        scatter(sgh, rgh, lgh, half, GROUPS["zgh"])
    relay(sgh, rgh, lgh, cgh, GROUPS["zgh"], 1)
    relay(sgh, rgh, lgh, cgh, GROUPS["zgh"], 0)
    copy(gx.at[k], gp.at[k], GROUPS["px"], GROUPS["px"], peer).start()
    reduce_and_share(sgu, rgu, agu, GROUPS["zgu"], GROUPS["agu"])
    reduce_and_share(sgh, rgh, agh, GROUPS["zgh"], GROUPS["agh"])

    first, last = (0, 5), (5, 8)

    def to_sibling(sums, kept, given, turn, name):
        def one(i):
            kept[i] = sums[rows(32 * i + 16 * (1 - k), 16), :].astype(BF16)
        lo, hi = (first, last)[turn]
        loop(lo, hi, one)
        some = pl.ds(lo, hi - lo)
        copy(kept.at[some], given.at[some], GROUPS[name] + turn, GROUPS[name] + turn, sib).start()

    def to_owners(sums, given, folded, landed, turn, name, base):
        lo, hi = (first, last)[turn]
        arrived(given.at[pl.ds(lo, hi - lo)], GROUPS[name] + turn)

        def one(step):
            q = 7 - step
            offset = lax.rem(2 * lax.rem(q, 4) + q // 4 - r + 8, 8)
            i = jnp.where(offset == 0, 0, jnp.where(offset <= 4, 2 * offset - 1, 16 - 2 * offset))

            @pl.when((i >= lo) & (i < hi))
            def _():
                tile = sums[rows(32 * i + 16 * k, 16), :] + given[i].astype(F32)
                for dx in (1, 0):
                    j = 2 * q + dx
                    block = fold(tile[8 * dx:8 * dx + 8]).astype(BF16)

                    @pl.when(j == 0)
                    def _():
                        landed[0] = block

                    @pl.when(j > 0)
                    def _():
                        folded[j] = block
                        to, slot = chip(j)
                        copy(folded.at[j], landed.at[slot], base + j, base + slot, to).start()
        loop(0, 8, one)

    def forward(turn):
        def one(i):
            gate, up = part(agu[group_of(ring(i))].astype(F32))
            hidden = gate * jax.nn.sigmoid(gate) * up
            hid[rows(32 * i, 32), :] = hidden[:, :448].astype(BF16)
        lo, hi = (first, last)[turn]
        loop(lo, hi, one)
        lines = slice(32 * lo, 32 * hi)
        lo_f[lines] = dot(hid[lines], wd[...])
        to_sibling(lo_f, lo_s, lo_i, turn, "lo_sib")

    def backward(turn):
        def one(i):
            q = group_of(ring(i))
            gate, up = part(agu[q].astype(F32))
            grad = jnp.concatenate(part(agh[q].astype(F32)), axis=0)
            sig = jax.nn.sigmoid(gate)
            both = join(grad * up * sig * (1.0 + gate * (1.0 - sig)), grad * (gate * sig)).astype(BF16)
            gl[rows(32 * i, 32), :] = both
            g[rows(32 * q, 32), :] = both
            copy(
                g.at[rows(32 * q, 32)], g.at[rows(256 + 32 * q, 32)], GROUPS["pg"] + q, GROUPS["pg"] + q, peer
            ).start()
        lo, hi = (first, last)[turn]
        loop(lo, hi, one)
        lines = slice(32 * lo, 32 * hi)
        gi_f[lines] = dot(gl[lines], wj[...])
        to_sibling(gi_f, gi_s, gi_i, turn, "gi_sib")

    pass_on(agu, GROUPS["agu"])
    come(agu, GROUPS["agu"], 1, 3)
    forward(0)
    pass_on(agh, GROUPS["agh"])
    come(agh, GROUPS["agh"], 1, 3)
    backward(0)
    arrived(gp.at[k], GROUPS["px"])
    copy(gp.at[k], gp.at[k], GROUPS["px_sib"], GROUPS["px_sib"], sib).start()
    to_owners(lo_f, lo_i, lo_t, lo_r, 0, "lo_sib", GROUPS["lo"])
    to_owners(gi_f, gi_i, gi_t, gi_r, 0, "gi_sib", GROUPS["gi"])
    come(agu, GROUPS["agu"], 5, 8)
    forward(1)
    to_owners(lo_f, lo_i, lo_t, lo_r, 1, "lo_sib", GROUPS["lo"])
    come(agh, GROUPS["agh"], 5, 8)
    backward(1)
    to_owners(gi_f, gi_i, gi_t, gi_r, 1, "gi_sib", GROUPS["gi"])

    arrived(gp.at[1 - k], GROUPS["px_sib"])
    loop(0, 8, lambda q: unfold(gp, x, 256, q))
    save_x = pltpu.make_async_copy(x, x_out, wsem.at[5])
    save_x.start()
    def drain(j):
        left(gx.at[k, 0], GROUPS["tok"] + j)
        left(gc.at[k, 0], GROUPS["cot"] + j)
        left(lo_t.at[j], GROUPS["lo"] + j)
        left(gi_t.at[j], GROUPS["gi"] + j)
    loop(1, 16, drain)

    def drain_row(i):
        left(sgu.at[0], GROUPS["zgu"] + i)
        left(sgh.at[0], GROUPS["zgh"] + i)
        left(agu.at[0], GROUPS["agu"] + i + 1)
        left(agh.at[0], GROUPS["agh"] + i + 1)
    loop(0, 7, drain_row)
    loop(0, 8, lambda q: left(g.at[rows(32 * q, 32)], GROUPS["pg"] + q))
    for half in range(2):
        left(gx.at[k, pl.ds(8 * half, 8)], GROUPS["tok_sib"] + half)
        left(gc.at[k, pl.ds(8 * half, 8)], GROUPS["cot_sib"] + half)
        lo, hi = (first, last)[half]
        left(lo_s.at[pl.ds(lo, hi - lo)], GROUPS["lo_sib"] + half)
        left(gi_s.at[pl.ds(lo, hi - lo)], GROUPS["gi_sib"] + half)
    left(gx.at[k], GROUPS["px"])
    left(gp.at[k], GROUPS["px_sib"])
    loop(1, 16, lambda j: arrived(lo_r.at[j], GROUPS["lo"] + j))
    save_lo = pltpu.make_async_copy(lo_r, lo_out, wsem.at[6])
    save_lo.start()
    loop(0, 8, lambda q: arrived(g.at[rows(256 + 32 * q, 32)], GROUPS["pg"] + q))
    save_g = pltpu.make_async_copy(g, g_out, wsem.at[7])
    save_g.start()

    loop(1, 16, lambda j: arrived(gi_r.at[j], GROUPS["gi"] + j))
    save_gi = pltpu.make_async_copy(gi_r, gi_out, wsem.at[8])
    save_gi.start()
    for save in (save_x, save_lo, save_g, save_gi):
        save.wait()


def finish(x_ref, g_ref, lo_ref, gi_ref, lo_out, gi_out, gg_out, gu_out):
    for parts, out in ((lo_ref, lo_out), (gi_ref, gi_out)):
        total = parts[0].astype(F32)
        for j in range(1, 16):
            total = total + parts[j].astype(F32)
        out[...] = jnp.concatenate([total[:8], total[8:]], axis=1).astype(BF16)
    grads = dot_tn(g_ref[...], x_ref[...]).astype(BF16)
    gg_out[:384] = grads[:384]
    gu_out[:384] = grads[384:768]
    gg_out[384:] = grads[768:832]
    gu_out[384:] = grads[832:]


def body(tokens, gate_weight, up_weight, down_weight, cotangent):
    vmem = pl.BlockSpec(memory_space=pltpu.VMEM)
    anywhere = pl.BlockSpec(memory_space=pl.ANY)
    scratch = [
        ((896, 1024), BF16), ((448, 1024), BF16),
        ((2, 16, 16, 512), BF16), ((2, 16, 16, 512), BF16), ((2, 16, 16, 512), BF16),
        ((512, 1024), BF16), ((256, 1024), BF16),
        ((8, 32, 896), BF16), ((4, 32, 896), BF16), ((3, 32, 896), BF16), ((2, 32, 896), BF16),
        ((8, 16, 896), BF16), ((4, 16, 896), BF16), ((3, 16, 896), BF16), ((2, 16, 896), BF16),
        ((8, 32, 896), BF16), ((8, 16, 896), BF16),
        ((256, 448), BF16), ((256, 896), BF16), ((512, 896), BF16),
        ((256, 1024), F32), ((256, 1024), F32),
        ((8, 16, 1024), BF16), ((8, 16, 1024), BF16), ((8, 16, 1024), BF16), ((8, 16, 1024), BF16),
        ((16, 16, 512), BF16), ((16, 16, 512), BF16), ((16, 16, 512), BF16), ((16, 16, 512), BF16),
    ]
    grant = 61 * 1024 * 1024
    x, g, lo, gi = pl.pallas_call(
        kernel,
        out_shape=(
            jax.ShapeDtypeStruct((512, 1024), BF16),
            jax.ShapeDtypeStruct((512, 896), BF16),
            jax.ShapeDtypeStruct((16, 16, 512), BF16),
            jax.ShapeDtypeStruct((16, 16, 512), BF16),
        ),
        in_specs=[vmem, anywhere, anywhere, anywhere, vmem],
        out_specs=(anywhere,) * 4,
        scratch_shapes=[pltpu.VMEM(shape, kind) for shape, kind in scratch]
        + [pltpu.SemaphoreType.DMA((N_SEM,)), pltpu.SemaphoreType.DMA((N_SEM,)), pltpu.SemaphoreType.DMA((9,))],
        compiler_params=pltpu.CompilerParams(collective_id=0, has_side_effects=True, vmem_limit_bytes=grant),
        cost_estimate=pl.CostEstimate(flops=1500000000, bytes_accessed=5000000, transcendentals=250000),
        name="swiglu_block",
    )(tokens, gate_weight.T, up_weight.T, down_weight, cotangent)
    layer_output, grad_input, grad_gate, grad_up = pl.pallas_call(
        finish,
        out_shape=(
            jax.ShapeDtypeStruct((8, 1024), BF16),
            jax.ShapeDtypeStruct((8, 1024), BF16),
            jax.ShapeDtypeStruct((448, 1024), BF16),
            jax.ShapeDtypeStruct((448, 1024), BF16),
        ),
        in_specs=[vmem] * 4,
        out_specs=(vmem,) * 4,
        compiler_params=pltpu.CompilerParams(vmem_limit_bytes=grant),
        cost_estimate=pl.CostEstimate(flops=940000000, bytes_accessed=4500000, transcendentals=0),
        name="finish",
    )(x, g, lo, gi)
    return layer_output, grad_input, grad_gate.T, grad_up.T


def solution(mesh):
    return jax.shard_map(
        body,
        mesh=mesh,
        in_specs=(
            P(("dp", "col"), "row"),
            P("row", "col"),
            P("row", "col"),
            P("col", "row"),
            P(("dp", "col"), "row"),
        ),
        out_specs=(
            P(("dp", "col"), "row"),
            P(("dp", "col"), "row"),
            P("row", "col"),
            P("row", "col"),
        ),
        check_vma=False,
    )
```
